32 devices in a mesh: il: 4 (over x, core), xl: 8 (over z, y).
Axes of the slice: x: 2, y: 2, z: 4, core: 2. Of those that a mesh axis runs over, the one named last changes fastest.
Arguments:
- traces: bfloat16 [245760, 128], P(('il', 'xl')), may hold values from -6 to 6
- filter_taps: float32 [12, 64], replicated, may hold values from -1.5 to 1.5
- slot_block: int32 [32, 32, 7], P(('il', 'xl')), may hold values from 0 to 59
- slot_cells: int32 [32, 32, 7, 128], P(('il', 'xl')), may hold values from -1 to 1535
- pair_count: int32 [32, 32], P(('il', 'xl')), may hold values from 0 to 7, as said below
Outputs:
- structure_tensor: float32 [6, 128, 384, 128], P(None, 'il', 'xl')
- adjoint_traces: float32 [245760, 128], P(('il', 'xl'))
The draws below stay inside these ranges and needn't reach their ends.
Inputs may be any that keep to these rules, and one draw needn't show every extreme that they name: Slots 0 to pair_count[e, d] - 1 of device e toward tile d are live; at most 7, and for some tiles every device sends 7 live slots.
All inputs are finite; a program needn't handle non-finite values.
Results may differ from the reference program's by a relative error of at most 0.0004.
The reference program's roundings to bfloat16 on the way count: a program that leaves them out, or rounds other values in their place, can miss the bound.
Values may be sent and summed in bfloat16 or wider, within the bound.
No kernel may reach another device: no remote copies, remote signals or barrier semaphores. Data moves between devices by JAX's collectives and lax.ppermute only.
A program may use at most 128 MiB of HBM per device.

```python
import jax
import jax.numpy as jnp
from jax import lax

NT = 128
TAPS = 64
NSURV = 12
ROWBLK = 128
BLK_SURV = 5
CIL = 32
CXL = 48
NDEV = 32
NBLK = 60
CAP = 7
CELLS = 1536
NIL = 128
NXL = 384
TRACES = 245760
N_IL = 4
N_XL = 8


def draw_slot_cells(key, part):
    first_key, second_key = jax.random.split(jax.random.fold_in(key, 11))
    cell_ids = jax.random.randint(first_key, (NDEV, NDEV, CAP, ROWBLK), 0, CELLS)
    dropped = jax.random.randint(second_key, (NDEV, NDEV, CAP, ROWBLK), 0, 4) == 0
    return jnp.where(dropped, -1, cell_ids).astype(jnp.int32)


def draw_pair_count(key, part):
    first_key, second_key = jax.random.split(jax.random.fold_in(key, 23))
    ranking = jax.random.permutation(first_key, NDEV)
    heavy = ranking < max(NDEV // 8, 1)
    light = jax.random.randint(second_key, (NDEV, NDEV), 0, CAP)
    return jnp.where(heavy[None, :], CAP, light).astype(jnp.int32)


def with_ends(values, stream_key, least, largest):
    index_at = [jax.random.randint(jax.random.fold_in(stream_key, axis), (), 0, length) for axis, length in enumerate(values.shape)]
    longest = values.shape.index(max(values.shape))
    neighbour = index_at[:longest] + [(index_at[longest] + 1) % values.shape[longest]] + index_at[longest + 1:]
    return values.at[tuple(index_at)].set(least).at[tuple(neighbour)].set(largest)


def level_of(own_key, shape, cuts, low, high):
    level = 1.0
    for position, parts in cuts:
        heights = jax.random.uniform(jax.random.fold_in(jax.random.fold_in(own_key, 6), position), (parts,), jnp.float32, low / len(cuts), high / len(cuts))
        level = level * jnp.repeat(jnp.exp(heights), shape[position] // parts).reshape((-1,) + (1,) * (len(shape) - 1 - position))
    return level


def noise(key, extent, spread, bound, cuts=(), kind=jnp.bfloat16):
    result = spread * jax.random.normal(key, extent, jnp.float32)
    if cuts:
        result = result * level_of(key, extent, cuts, -0.22, 0.18)
    return jnp.clip(result, -bound, bound).astype(kind)


def setup_inputs(seed: int = 0) -> dict:
    splits = jax.random.split(jax.random.key(seed), 6)
    traces = noise(splits[0], (TRACES, NT), 1.0, 6.0, ((0, 32),))
    filter_taps = noise(splits[1], (NSURV, TAPS), 0.25, 1.5, (), jnp.float32)
    slot_block = with_ends(jax.random.randint(splits[2], (NDEV, NDEV, CAP), 0, NBLK), jax.random.fold_in(splits[2], 1), 0, NBLK - 1).astype(jnp.int32)
    slot_cells = draw_slot_cells(jax.random.fold_in(splits[5], 71), 0)
    pair_count = draw_pair_count(jax.random.fold_in(splits[5], 71), 0)
    return {"traces": traces, "filter_taps": filter_taps, "slot_block": slot_block, "slot_cells": slot_cells, "pair_count": pair_count}


def filter_matrices(filter_taps, samples):
    lag_table = jnp.arange(samples, dtype=jnp.int32)[None, :] - jnp.arange(samples, dtype=jnp.int32)[:, None]
    tap_count = filter_taps.shape[1]
    inside = (lag_table >= 0) & (lag_table < tap_count)
    picked = filter_taps[:, jnp.clip(lag_table, 0, tap_count - 1)]
    return jnp.where(inside[None], picked, 0.0).astype(jnp.bfloat16)


def smooth_box(values):
    padded = jnp.pad(values, ((1, 1), (1, 1), (0, 0)))
    box_total = jnp.zeros_like(values)
    for row_shift in range(3):
        for col_shift in range(3):
            box_total = box_total + padded[row_shift:row_shift + values.shape[0], col_shift:col_shift + values.shape[1]]
    return box_total / 9.0


def reference(traces, filter_taps, slot_block, slot_cells, pair_count):
    matrices = filter_matrices(filter_taps, NT)
    by_survey = traces.reshape(NDEV, NSURV, BLK_SURV * ROWBLK, NT)

    def filter_survey(survey):
        inputs = by_survey[:, survey].reshape(NDEV * BLK_SURV * ROWBLK, NT)
        return jnp.dot(inputs, matrices[survey], preferred_element_type=jnp.float32).astype(jnp.bfloat16)

    filtered = lax.map(filter_survey, jnp.arange(NSURV, dtype=jnp.int32))
    filtered = filtered.reshape(NSURV, NDEV, BLK_SURV, ROWBLK, NT).transpose(1, 0, 2, 3, 4).reshape(NDEV, NBLK, ROWBLK, NT)
    slot_live = jnp.arange(CAP, dtype=jnp.int32)[None, None, :] < pair_count[:, :, None]
    live_cells = jnp.where(slot_live[..., None], slot_cells, -1)
    sources = jnp.arange(NDEV, dtype=jnp.int32)

    def stack_tile(target):
        blocks = filtered[sources[:, None], slot_block[:, target, :]]
        cell_ids = live_cells[:, target]
        segment = jnp.where(cell_ids >= 0, cell_ids, CELLS).reshape(-1)
        values = blocks.reshape(-1, NT).astype(jnp.float32)
        stacked = jax.ops.segment_sum(values, segment, CELLS + 1)[:CELLS]
        fold_counts = jax.ops.segment_sum(jnp.ones(segment.shape, jnp.float32), segment, CELLS + 1)[:CELLS]
        return stacked / jnp.maximum(fold_counts, 1.0)[:, None]

    stack_image = lax.map(stack_tile, sources)
    image_half = stack_image.astype(jnp.bfloat16)

    def adjoint_source(source):
        blocks = filtered[source][slot_block[source]]
        cell_ids = live_cells[source]
        is_valid = cell_ids >= 0
        returned = image_half[sources[:, None, None], jnp.where(is_valid, cell_ids, 0)]
        difference = jnp.where(is_valid[..., None], blocks.astype(jnp.float32) - returned.astype(jnp.float32), 0.0)
        residual = jax.ops.segment_sum(difference.reshape(NDEV * CAP, ROWBLK, NT), slot_block[source].reshape(-1), NBLK)
        residual_half = residual.astype(jnp.bfloat16).reshape(NSURV, BLK_SURV * ROWBLK, NT)
        adjoint = jnp.einsum("srt,sut->sru", residual_half.astype(jnp.float32), matrices.astype(jnp.float32), precision=lax.Precision.HIGHEST)
        return adjoint.reshape(NBLK * ROWBLK, NT)

    adjoint_traces = lax.map(adjoint_source, sources).reshape(TRACES, NT)
    grid_image = stack_image.reshape(N_IL, N_XL, CIL, CXL, NT).transpose(0, 2, 1, 3, 4).reshape(NIL, NXL, NT)
    padded = jnp.pad(grid_image, 1)
    grad_il = (padded[2:, 1:-1, 1:-1] - padded[:-2, 1:-1, 1:-1]) * 0.5
    grad_xl = (padded[1:-1, 2:, 1:-1] - padded[1:-1, :-2, 1:-1]) * 0.5
    grad_time = (padded[1:-1, 1:-1, 2:] - padded[1:-1, 1:-1, :-2]) * 0.5
    factor_pairs = ((grad_il, grad_il), (grad_xl, grad_xl), (grad_time, grad_time), (grad_il, grad_xl), (grad_il, grad_time), (grad_xl, grad_time))
    structure_tensor = jnp.stack([smooth_box(left_part * right_part) for left_part, right_part in factor_pairs])
    return (structure_tensor, adjoint_traces)
```

```python
import functools

import jax
import jax.numpy as jnp
from jax import lax
from jax.experimental import pallas as pl
from jax.experimental.pallas import tpu as pltpu
from jax.sharding import Mesh
from jax.sharding import PartitionSpec as P

CIL = 32
CXL = 48
CELLS = CIL * CXL
HALF = CELLS // 2
MIB = 1 << 20
IN_SMEM = pl.BlockSpec(memory_space=pltpu.SMEM)
IN_VMEM = pl.BlockSpec(memory_space=pltpu.VMEM)
IN_ANY = pl.BlockSpec(memory_space=pl.ANY)


def hot(cells, shape, axis):
    line = lax.broadcasted_iota(jnp.int32, shape, axis)
    return jnp.where(line == cells, 1.0, 0.0).astype(jnp.bfloat16)


def lower(cells):
    return jnp.where(cells >= HALF, cells - HALF, cells)


def filter_kernel(taps, low_in, high_in, low_out, high_out, matrices):
    step = pl.program_id(0)
    samples = low_in.shape[2]
    row = lax.broadcasted_iota(jnp.int32, (samples, samples), 0)
    col = lax.broadcasted_iota(jnp.int32, (samples, samples), 1)
    for part, (source, target) in enumerate(((low_in, low_out), (high_in, high_out))):
        survey = step + part * pl.num_programs(0)
        line = jnp.broadcast_to(taps[survey], (samples, samples))
        band = pltpu.roll(line, 0, 1, stride=1, stride_axis=0)
        matrix = jnp.where(col >= row, band, 0.0).astype(jnp.bfloat16)
        matrices[part, 0] = matrix
        target[0] = jnp.dot(source[0], matrix, preferred_element_type=jnp.float32).astype(
            jnp.bfloat16
        )


def filter_call(traces, filter_taps):
    surveys, tap_count = filter_taps.shape
    samples = traces.shape[1]
    rows = traces.shape[0] // surveys
    steps = surveys // 2
    by_survey = traces.reshape(surveys, rows, samples)
    taps = jnp.pad(filter_taps, ((0, 0), (0, samples - tap_count))).reshape(surveys, 1, samples)
    low, high, matrices = pl.pallas_call(
        filter_kernel,
        grid=(steps,),
        in_specs=[
            pl.BlockSpec((surveys, 1, samples), lambda i: (0, 0, 0)),
            pl.BlockSpec((1, rows, samples), lambda i: (i, 0, 0)),
            pl.BlockSpec((1, rows, samples), lambda i: (i + steps, 0, 0)),
        ],
        out_specs=[
            pl.BlockSpec((1, rows, samples), lambda i: (i, 0, 0)),
            pl.BlockSpec((1, rows, samples), lambda i: (i, 0, 0)),
            pl.BlockSpec((2, 1, samples, samples), lambda i: (0, i, 0, 0)),
        ],
        out_shape=[
            jax.ShapeDtypeStruct((steps, rows, samples), jnp.bfloat16),
            jax.ShapeDtypeStruct((steps, rows, samples), jnp.bfloat16),
            jax.ShapeDtypeStruct((2, steps, samples, samples), jnp.bfloat16),
        ],
        name="filter",
    )(taps, by_survey, by_survey)
    return (
        low.reshape(steps * rows, samples),
        high.reshape(steps * rows, samples),
        matrices.reshape(surveys, samples, samples),
    )


def stack_kernel(sources, tiles, block_rows, first, order, counts, blocks, cells, *refs):
    group = 8
    pieces = refs[: 2 * sources]
    refs = refs[2 * sources :]
    if first:
        out, held, live, sems = refs
    else:
        before, out, held, live, sems = refs
    rows = pieces[0].shape[0]
    copies = [
        pltpu.make_async_copy(piece, held.at[pl.ds(i * rows, rows)], sems.at[i])
        for i, piece in enumerate(pieces)
    ]
    for copy in copies:
        copy.start()
    out[...] = jnp.zeros_like(out) if first else before[...]
    for copy in copies:
        copy.wait()

    def tile_step(tile, unused):
        def add_source(source, n):
            base = order[source] * tiles + tile

            def add_slot(c, n):
                live[n] = base * 8 + c
                live[n + 256] = blocks[base * 8 + c] * block_rows + source * (2 * rows)
                return n + 1

            return lax.fori_loop(0, counts[base], add_slot, n)

        n = lax.fori_loop(0, sources, add_source, 0)

        def one_group(g, unused):
            picked = []
            for i in range(group):
                at = g * group + i
                entry = live[jnp.minimum(at, n - 1)]
                picked.append(jnp.where(at < n, cells[pl.ds(entry, 1), :], -1))
            columns = jnp.concatenate(picked, axis=0).T
            data = []
            for i in range(group):
                start = live[256 + jnp.minimum(g * group + i, n - 1)]
                block = held[pl.ds(pl.multiple_of(start, block_rows), block_rows), :]
                upper = columns[:, i : i + 1] >= HALF
                zero = jnp.zeros_like(block)
                data.append(
                    jnp.concatenate(
                        [jnp.where(upper, zero, block), jnp.where(upper, block, zero)], axis=1
                    )
                )
            data = jnp.concatenate(data, axis=0)
            line = jnp.concatenate(picked, axis=1)
            width = line.shape[1]
            selector = hot(lower(line), (HALF, width), 0)
            out[tile, :HALF] += jnp.dot(selector, data, preferred_element_type=jnp.float32)
            inline = ((line >> 4) * 171) >> 9
            cross = line - CXL * inline
            out[tile, HALF:, :128] += lax.dot_general(
                hot(cross, (CXL, width), 0),
                hot(inline, (128, width), 0),
                (((1,), (1,)), ((), ())),
                preferred_element_type=jnp.float32,
            )
            return 0

        lax.fori_loop(0, (n + group - 1) // group, one_group, 0)
        return 0

    lax.fori_loop(0, tiles, tile_step, 0)


def stack_call(order, counts, blocks, cells, pieces, before, tiles, block_rows):
    sources = len(pieces) // 2
    first = before is None
    rows = pieces[0].shape[0]
    extra = [] if first else [before]
    return pl.pallas_call(
        functools.partial(stack_kernel, sources, tiles, block_rows, first),
        out_shape=jax.ShapeDtypeStruct((tiles, HALF + CXL, 256), jnp.float32),
        in_specs=[IN_SMEM] * 3 + [IN_VMEM] + [IN_ANY] * len(pieces) + [IN_VMEM] * len(extra),
        out_specs=IN_VMEM,
        scratch_shapes=[
            pltpu.VMEM((sources * 2 * rows, 128), jnp.bfloat16),
            pltpu.SMEM((512,), jnp.int32),
            pltpu.SemaphoreType.DMA((len(pieces),)),
        ],
        compiler_params=pltpu.CompilerParams(vmem_limit_bytes=40 * MIB),
        cost_estimate=pl.CostEstimate(
            flops=sources * tiles * 7 * 2 * HALF * 128 * 256,
            bytes_accessed=len(pieces) * rows * 256 + 8 * MIB,
            transcendentals=0,
        ),
        name="stack",
    )(order, counts, blocks, cells, *pieces, *extra)


def image_kernel(stack, image, packed):
    for a in range(CIL):
        fold = jnp.maximum(stack[HALF:, a : a + 1], 1.0)
        side = a // (CIL // 2)
        low = (a - side * (CIL // 2)) * CXL
        value = stack[low : low + CXL, side * 128 : side * 128 + 128] / fold
        image[a * CXL : (a + 1) * CXL] = value
        packed[low : low + CXL, side * 128 : side * 128 + 128] = value.astype(jnp.bfloat16)


def image_call(stack):
    return pl.pallas_call(
        image_kernel,
        out_shape=[
            jax.ShapeDtypeStruct((CELLS, 128), jnp.float32),
            jax.ShapeDtypeStruct((HALF, 256), jnp.bfloat16),
        ],
        in_specs=[IN_VMEM],
        out_specs=[IN_VMEM, IN_VMEM],
        name="image",
    )(stack)


def read_kernel(tiles, block_rows, first, order, counts, blocks, cells, low, high, *refs):
    group = 4
    images = refs[:tiles]
    refs = refs[tiles:]
    if first:
        out, held, own, sems = refs
    else:
        before, out, held, own, sems = refs
    rows = low.shape[0]
    copies = [
        pltpu.make_async_copy(image, held.at[i], sems.at[i]) for i, image in enumerate(images)
    ]
    copies += [
        pltpu.make_async_copy(part, own.at[pl.ds(i * rows, rows)], sems.at[tiles + i])
        for i, part in enumerate((low, high))
    ]
    for copy in copies:
        copy.start()
    out[...] = jnp.zeros_like(out) if first else before[...]
    for copy in copies:
        copy.wait()

    def tile_step(j, unused):
        tile = order[j]
        n = counts[tile]
        columns = cells[pl.ds(pl.multiple_of(tile * 8, 8), 8), :].T
        for g in range(8 // group):

            @pl.when(n > g * group)
            def _():
                picks = [columns[:, g * group + i : g * group + i + 1] for i in range(group)]
                selector = jnp.concatenate(
                    [hot(lower(pick), (block_rows, HALF), 1) for pick in picks], axis=0
                )
                got = jnp.dot(selector, held[j], preferred_element_type=jnp.float32)
                for i, pick in enumerate(picks):
                    start = blocks[tile * 8 + g * group + i] * block_rows
                    here = pl.ds(pl.multiple_of(start, block_rows), block_rows)
                    part = got[i * block_rows : (i + 1) * block_rows]
                    value = jnp.where(pick >= HALF, part[:, 128:], part[:, :128])
                    mine = own[here, :].astype(jnp.float32)
                    out[here, :] += jnp.where(pick >= 0, mine, 0.0) - value

        return 0

    lax.fori_loop(0, tiles, tile_step, 0)


def read_call(order, counts, blocks, cells, low, high, images, before, block_rows):
    tiles = len(images)
    first = before is None
    rows = low.shape[0]
    extra = [] if first else [before]
    return pl.pallas_call(
        functools.partial(read_kernel, tiles, block_rows, first),
        out_shape=jax.ShapeDtypeStruct((2 * rows, 128), jnp.float32),
        in_specs=[IN_SMEM] * 3 + [IN_VMEM] + [IN_ANY] * (2 + tiles) + [IN_VMEM] * len(extra),
        out_specs=IN_VMEM,
        scratch_shapes=[
            pltpu.VMEM((tiles, HALF, 256), jnp.bfloat16),
            pltpu.VMEM((2 * rows, 128), jnp.bfloat16),
            pltpu.SemaphoreType.DMA((tiles + 2,)),
        ],
        compiler_params=pltpu.CompilerParams(vmem_limit_bytes=40 * MIB),
        cost_estimate=pl.CostEstimate(
            flops=tiles * 7 * 2 * HALF * 128 * 256,
            bytes_accessed=16 * MIB,
            transcendentals=0,
        ),
        name="read",
    )(order, counts, blocks, cells, low, high, *images, *extra)


def adjoint_kernel(residual, matrix, out):
    out[0] = lax.dot_general(
        residual[0].astype(jnp.bfloat16),
        matrix[0],
        (((1,), (1,)), ((), ())),
        preferred_element_type=jnp.float32,
    )


def adjoint_call(residual, matrices):
    surveys, samples, unused = matrices.shape
    rows = residual.shape[0] // surveys
    return pl.pallas_call(
        adjoint_kernel,
        grid=(surveys,),
        in_specs=[
            pl.BlockSpec((1, rows, samples), lambda i: (i, 0, 0)),
            pl.BlockSpec((1, samples, samples), lambda i: (i, 0, 0)),
        ],
        out_specs=pl.BlockSpec((1, rows, samples), lambda i: (i, 0, 0)),
        out_shape=jax.ShapeDtypeStruct((surveys, rows, samples), jnp.float32),
        name="adjoint",
    )(residual.reshape(surveys, rows, samples), matrices).reshape(residual.shape)


def with_halo(block, sides, width):
    for axis, count, dim in sides:
        forward = [(i, i + 1) for i in range(count - 1)]
        backward = [(target, source) for source, target in forward]
        low = lax.ppermute(
            lax.slice_in_dim(block, block.shape[dim] - width, None, axis=dim), axis, forward
        )
        high = lax.ppermute(lax.slice_in_dim(block, 0, width, axis=dim), axis, backward)
        block = jnp.concatenate([low, block, high], axis=dim)
    return block


def cycle_box(values, rows_out, cols_out):
    box_total = jnp.zeros((rows_out, cols_out, values.shape[2]), jnp.float32)
    for row_shift in range(3):
        for col_shift in range(3):
            box_total = (
                box_total
                + values[row_shift : row_shift + rows_out, col_shift : col_shift + cols_out]
            )
    return box_total / 9.0


def tensor(tile_image, il, xl):
    axis_il, count_il, at_il = il
    axis_xl, count_xl, at_xl = xl
    padded = with_halo(tile_image, ((axis_il, count_il, 0), (axis_xl, count_xl, 1)), 2)
    padded_time = jnp.pad(padded, ((0, 0), (0, 0), (1, 1)))
    grad_il = (padded[2:, 1:-1] - padded[:-2, 1:-1]) * 0.5
    grad_xl = (padded[1:-1, 2:] - padded[1:-1, :-2]) * 0.5
    grad_time = (padded_time[1:-1, 1:-1, 2:] - padded_time[1:-1, 1:-1, :-2]) * 0.5
    rows_il = at_il * CIL + jnp.arange(CIL + 2, dtype=jnp.int32) - 1
    rows_xl = at_xl * CXL + jnp.arange(CXL + 2, dtype=jnp.int32) - 1
    inside_il = ((rows_il >= 0) & (rows_il < CIL * count_il)).astype(jnp.float32)
    inside_xl = ((rows_xl >= 0) & (rows_xl < CXL * count_xl)).astype(jnp.float32)
    cycle_mask = inside_il[:, None, None] * inside_xl[None, :, None]
    factor_pairs = (
        (grad_il, grad_il),
        (grad_xl, grad_xl),
        (grad_time, grad_time),
        (grad_il, grad_xl),
        (grad_il, grad_time),
        (grad_xl, grad_time),
    )
    return jnp.stack(
        [
            cycle_box(left_part * right_part * cycle_mask, CIL, CXL)
            for left_part, right_part in factor_pairs
        ]
    )


SWAP = [(0, 1), (1, 0)]


def over(axis, value):
    return lax.ppermute(value, axis, SWAP)


def along_z(value, step):
    return lax.ppermute(value, "z", [(i, (i + step) % 4) for i in range(4)])


def local_planes(traces, filter_taps, slot_block, slot_cells, pair_count):
    row_block = slot_cells.shape[3]
    capacity = slot_block.shape[2]
    x, core, z, y = (lax.axis_index(name) for name in ("x", "c", "z", "y"))

    def place(at_x, at_core, at_z, at_y):
        return ((at_x * 2 + at_core) * 4 + at_z) * 2 + at_y

    low, high, matrices = filter_call(traces, filter_taps)

    slot_live = jnp.arange(capacity, dtype=jnp.int32)[None, :] < pair_count[0][:, None]
    out_cells = jnp.where(slot_live[:, :, None], slot_cells[0], -1)
    numbers = jnp.concatenate([slot_block[0], pair_count[0][:, None]], axis=1)
    numbers = jnp.pad(numbers, ((0, 0), (0, row_block - 8)))
    slots = jnp.concatenate([out_cells, numbers[:, None, :]], axis=1)
    by_column = slots.reshape(2, 2, 4, 2, 8, row_block).transpose(0, 1, 3, 2, 4, 5)
    arrived = lax.all_to_all(
        by_column.reshape(8, 4, 8, row_block), ("x", "c", "y"), 0, 0, tiled=True
    )
    in_cells = arrived.reshape(256, row_block)
    in_numbers = arrived[:, :, 7, :8].reshape(32, 8)
    in_counts = in_numbers[:, 7]
    in_blocks = in_numbers.reshape(256)

    x0, y1 = over("x", low), over("y", high)
    x1, y0 = over("x", high), over("y", low)
    d0, d1 = over("y", x0), over("x", y1)

    def column(*sources):
        return jnp.stack([(at_x * 2 + at_core) * 2 + at_y for at_x, at_core, at_y in sources])

    other = 1 - core
    stack = None
    for pieces, spots in (
        (([low, high],), ((x, y),)),
        (([x0, x1], [y0, y1]), ((1 - x, y), (x, 1 - y))),
        (([d0, d1],), ((1 - x, 1 - y),)),
    ):
        operands, sources = [], []
        for pair, (at_x, at_y) in zip(pieces, spots, strict=True):
            operands += pair + [over("c", part) for part in pair]
            sources += [(at_x, core, at_y), (at_x, other, at_y)]
        stack = stack_call(
            column(*sources), in_counts, in_blocks, in_cells, operands, stack, 4, row_block
        )
    total = lax.psum_scatter(stack, "z", scatter_dimension=0, tiled=True)[0]
    image, packed = image_call(total)

    structure_tensor = tensor(
        image.reshape(CIL, CXL, 128),
        (("x", "c"), 4, x * 2 + core),
        (("z", "y"), 8, z * 2 + y),
    )

    own_counts = pair_count[0]
    own_blocks = numbers[:, :8].reshape(256)
    own_cells = jnp.pad(out_cells, ((0, 0), (0, 1), (0, 0)), constant_values=-1)
    own_cells = own_cells.reshape(256, row_block)
    residual = None
    layers = [(packed, 0)] + [(along_z(packed, step), step) for step in (1, 3, 2)]
    for turn, (layer, step) in enumerate(layers):
        from_x, from_y = over("x", layer), over("y", layer)
        diagonal = over("y", from_x) if turn % 2 == 0 else over("x", from_y)
        mine = [layer, from_x, from_y, diagonal]
        spots = [(x, y), (1 - x, y), (x, 1 - y), (1 - x, 1 - y)]
        images = mine + [over("c", part) for part in mine]
        at_z = lax.rem(z + 4 - step, 4)
        order = jnp.stack(
            [place(at_x, core, at_z, at_y) for at_x, at_y in spots]
            + [place(at_x, other, at_z, at_y) for at_x, at_y in spots]
        )
        residual = read_call(
            order, own_counts, own_blocks, own_cells, low, high, images, residual, row_block
        )
    return (structure_tensor, adjoint_call(residual, matrices))


def filter_matrices(filter_taps, samples):
    lag_table = (
        jnp.arange(samples, dtype=jnp.int32)[None, :]
        - jnp.arange(samples, dtype=jnp.int32)[:, None]
    )
    tap_count = filter_taps.shape[1]
    inside = (lag_table >= 0) & (lag_table < tap_count)
    picked = filter_taps[:, jnp.clip(lag_table, 0, tap_count - 1)]
    return jnp.where(inside[None], picked, 0.0).astype(jnp.bfloat16)


def local(traces, filter_taps, slot_block, slot_cells, pair_count):
    count_il = lax.axis_size("il")
    count_xl = lax.axis_size("xl")
    devices = count_il * count_xl
    samples = traces.shape[1]
    row_block = slot_cells.shape[3]
    capacity = slot_block.shape[2]
    surveys = filter_taps.shape[0]
    blocks_here = traces.shape[0] // row_block
    cell_count = CIL * CXL
    group_size = 16
    slot_total = devices * capacity
    group_count = slot_total // group_size
    matrices = filter_matrices(filter_taps, samples)
    by_survey = traces.reshape(surveys, blocks_here // surveys * row_block, samples)
    filtered = jnp.einsum("sru,sut->srt", by_survey, matrices, preferred_element_type=jnp.float32)
    filtered = filtered.astype(jnp.bfloat16).reshape(blocks_here, row_block, samples)
    block_ids = slot_block[0].reshape(-1)
    outgoing = jnp.take(filtered, block_ids, axis=0).reshape(devices, capacity, row_block, samples)
    slot_live = jnp.arange(capacity, dtype=jnp.int32)[None, :] < pair_count[0][:, None]
    out_cells = jnp.where(slot_live[:, :, None], slot_cells[0], -1)
    incoming, in_cells = (
        lax.all_to_all(outgoing, ("il", "xl"), split_axis=0, concat_axis=0, tiled=True),
        lax.all_to_all(out_cells, ("il", "xl"), split_axis=0, concat_axis=0, tiled=True),
    )
    incoming = incoming.reshape(slot_total, row_block, samples)
    in_cells = in_cells.reshape(slot_total, row_block)
    cell_line = jnp.arange(cell_count, dtype=jnp.int32)

    def one_hot(group_cells):
        return (cell_line[:, None] == group_cells.reshape(1, -1)).astype(jnp.bfloat16)

    def add_group(running, group_blocks, group_cells):
        stacked, fold_counts = running
        selector = one_hot(group_cells)
        stacked = stacked + jnp.dot(
            selector, group_blocks.reshape(-1, samples), preferred_element_type=jnp.float32
        )
        fold_counts = fold_counts + jnp.sum(selector, axis=1, dtype=jnp.float32)
        return (stacked, fold_counts)

    initial = (jnp.zeros((cell_count, samples), jnp.float32), jnp.zeros((cell_count,), jnp.float32))

    def scan_step(running, scan_item):
        return (add_group(running, scan_item[0], scan_item[1]), None)

    (stacked, fold_counts), unused = lax.scan(
        scan_step,
        initial,
        (
            incoming.reshape(group_count, group_size, row_block, samples),
            in_cells.reshape(group_count, group_size, row_block),
        ),
    )
    stack_image = stacked / jnp.maximum(fold_counts, 1.0)[:, None]
    image_half = stack_image.astype(jnp.bfloat16)

    def read_group(group_cells):
        selector = one_hot(group_cells)
        picked = lax.dot_general(
            selector, image_half, (((0,), (0,)), ((), ())), preferred_element_type=jnp.float32
        )
        return picked.astype(jnp.bfloat16).reshape(group_size, row_block, samples)

    answer = lax.map(read_group, in_cells.reshape(group_count, group_size, row_block)).reshape(
        slot_total, row_block, samples
    )
    returned = lax.all_to_all(
        answer.reshape(devices, capacity, row_block, samples),
        ("il", "xl"),
        split_axis=0,
        concat_axis=0,
        tiled=True,
    )
    returned = returned.reshape(slot_total, row_block, samples)
    out_valid = (out_cells >= 0).reshape(slot_total, row_block, 1)
    zero_half = jnp.zeros((), jnp.bfloat16)
    sent_part = jnp.where(out_valid, outgoing.reshape(slot_total, row_block, samples), zero_half)
    back_part = jnp.where(out_valid, returned, zero_half)
    selector_rows = (
        block_ids[:, None] == jnp.arange(blocks_here, dtype=jnp.int32)[None, :]
    ).astype(jnp.bfloat16)
    residual = jnp.einsum(
        "sb,sit->bit", selector_rows, sent_part, preferred_element_type=jnp.float32
    )
    residual = residual - jnp.einsum(
        "sb,sit->bit", selector_rows, back_part, preferred_element_type=jnp.float32
    )
    residual_half = residual.astype(jnp.bfloat16).reshape(surveys, -1, samples)
    adjoint_traces = jnp.einsum(
        "srt,sut->sru", residual_half, matrices, preferred_element_type=jnp.float32
    ).reshape(traces.shape)
    structure_tensor = tensor(
        stack_image.reshape(CIL, CXL, samples),
        ("il", count_il, lax.axis_index("il")),
        ("xl", count_xl, lax.axis_index("xl")),
    )
    return (structure_tensor, adjoint_traces)


def solution(mesh):
    inner, names, body = mesh, (("il",), ("xl",)), local
    if mesh.devices.shape == (4, 8):
        inner = Mesh(mesh.devices.reshape(2, 2, 4, 2), ("x", "c", "z", "y"))
        names, body = (("x", "c"), ("z", "y")), local_planes
    il, xl = names
    both = il + xl
    return jax.shard_map(
        body,
        mesh=inner,
        in_specs=(
            P(both, None),
            P(),
            P(both, None, None),
            P(both, None, None, None),
            P(both, None),
        ),
        out_specs=(P(None, il, xl, None), P(both, None)),
        check_vma=False,
    )
```

```python
import functools

import jax
import jax.numpy as jnp
from jax import lax
from jax.experimental import pallas as pl
from jax.experimental.pallas import tpu as pltpu
from jax.sharding import Mesh
from jax.sharding import PartitionSpec as P

CIL = 32
CXL = 48
CELLS = CIL * CXL
QUARTER = CELLS // 4
FOLD = CXL // 3
MIB = 1 << 20
IN_SMEM = pl.BlockSpec(memory_space=pltpu.SMEM)
IN_VMEM = pl.BlockSpec(memory_space=pltpu.VMEM)
IN_ANY = pl.BlockSpec(memory_space=pl.ANY)


def hot(cells, shape, axis):
    line = lax.broadcasted_iota(jnp.int32, shape, axis)
    return jnp.where(line == cells, 1.0, 0.0).astype(jnp.bfloat16)


def quarter_of(cells):
    return sum((cells >= q * QUARTER).astype(jnp.int32) for q in (1, 2, 3))


def low_lanes(shape):
    return lax.broadcasted_iota(jnp.int32, shape, len(shape) - 1) < 64


def swap_lanes(value):
    return pltpu.roll(value, 64, 1)


def tie(value, *tokens):
    def kernel(*refs):
        pass

    return pl.pallas_call(
        kernel,
        out_shape=jax.ShapeDtypeStruct(value.shape, value.dtype),
        in_specs=[IN_ANY] * (1 + len(tokens)),
        out_specs=IN_ANY,
        input_output_aliases={0: 0},
        name="tie",
    )(value, *tokens)


def filter_kernel(half, taps, source, *targets):
    each, rows, samples = source.shape
    row = lax.broadcasted_iota(jnp.int32, (samples, samples), 0)
    col = lax.broadcasted_iota(jnp.int32, (samples, samples), 1)
    for i in range(each):
        line = jnp.broadcast_to(taps[i], (samples, samples))
        band = pltpu.roll(line, 0, 1, stride=1, stride_axis=0)
        matrix = jnp.where(col >= row, band, 0.0).astype(jnp.bfloat16)
        value = jnp.dot(source[i], matrix, preferred_element_type=jnp.float32)
        if half == 0:
            targets[1][i] = matrix
        else:
            targets[1][i] = value.astype(jnp.bfloat16)
        for block in range(rows // 128):
            top = value[block * 128 : block * 128 + 64]
            bottom = value[block * 128 + 64 : block * 128 + 128]
            left = low_lanes(top.shape)
            if half == 0:
                packed = jnp.where(left, top, swap_lanes(bottom))
            else:
                packed = jnp.where(left, swap_lanes(top), bottom)
            targets[0][i, block * 64 : block * 64 + 64] = packed.astype(jnp.bfloat16)


def filter_call(half, traces, taps):
    surveys, unused, samples = taps.shape
    rows = traces.shape[0] // surveys
    each = 3
    second = (each, samples, samples) if half == 0 else (each, rows, samples)
    return pl.pallas_call(
        functools.partial(filter_kernel, half),
        grid=(surveys // each,),
        in_specs=[
            pl.BlockSpec((each, 1, samples), lambda i: (i, 0, 0)),
            pl.BlockSpec((each, rows, samples), lambda i: (i, 0, 0)),
        ],
        out_specs=[
            pl.BlockSpec((each, rows // 2, samples), lambda i: (i, 0, 0)),
            pl.BlockSpec(second, lambda i: (i, 0, 0)),
        ],
        out_shape=[
            jax.ShapeDtypeStruct((surveys, rows // 2, samples), jnp.bfloat16),
            jax.ShapeDtypeStruct((surveys,) + second[1:], jnp.bfloat16),
        ],
        name=f"filter_{half}",
    )(taps, traces.reshape(surveys, rows, samples))


def stack_kernel(spec, tile_order, source_order, counts, blocks, cells, *refs):
    sizes, sources, tiles, with_fold, first, last = spec
    group = 8
    pieces = refs[: len(sizes)]
    refs = refs[len(sizes) :]
    if not first:
        before, refs = refs[0], refs[1:]
    outs = refs[: tiles if last else 1]
    held, total, live, sems = refs[len(outs) :]
    copies = []
    start = 0
    for i, rows in enumerate(sizes):
        copies.append(
            pltpu.make_async_copy(pieces[i], held.at[pl.ds(start, rows)], sems.at[i])
        )
        start += rows
    per_source = start // sources
    for copy in copies:
        copy.start()
    total[...] = jnp.zeros_like(total) if first else before[...]
    for copy in copies:
        copy.wait()

    def tile_step(tile, unused):
        def add_source(source, n):
            base = source_order[source] * tiles + tile_order[tile]

            def add_slot(c, n):
                live[n] = base * 8 + c
                live[n + 128] = blocks[base * 8 + c] * 64 + source * per_source
                return n + 1

            return lax.fori_loop(0, counts[base], add_slot, n)

        n = lax.fori_loop(0, sources, add_source, 0)

        def one_group(g, unused):
            picked = []
            for i in range(group):
                at = g * group + i
                entry = live[jnp.minimum(at, n - 1)]
                picked.append(jnp.where(at < n, cells[pl.ds(entry, 1), :], -1))
            rows = jnp.concatenate(picked, axis=0)
            columns = quarter_of(rows).T
            data = []
            left = low_lanes((64, 128))
            lane_group = 1 - low_lanes((128, 128)).astype(jnp.int32)
            for i in range(group):
                at = live[128 + jnp.minimum(g * group + i, n - 1)]
                block = held[pl.ds(pl.multiple_of(at, 64), 64), :].astype(jnp.float32)
                turned = swap_lanes(block)
                both = jnp.concatenate(
                    [jnp.where(left, block, turned), jnp.where(left, turned, block)], axis=0
                )
                spot = columns[:, i : i + 1] - lane_group
                data.append(
                    jnp.concatenate(
                        [jnp.where(spot == 0, both, 0.0), jnp.where(spot == 2, both, 0.0)], axis=1
                    ).astype(jnp.bfloat16)
                )
            data = jnp.concatenate(data, axis=0)
            line = jnp.concatenate(picked, axis=1)
            width = line.shape[1]
            selector = hot(line - QUARTER * quarter_of(line), (QUARTER, width), 0)
            total[tile, :QUARTER] += jnp.dot(selector, data, preferred_element_type=jnp.float32)
            if with_fold:
                inline = ((line >> 4) * 171) >> 9
                cross = line - CXL * inline
                row = jnp.where(line >= 0, cross & 15, -1)
                lane = inline + 32 * (cross >> 4)
                total[tile, QUARTER:, :128] += lax.dot_general(
                    hot(row, (FOLD, width), 0),
                    hot(lane, (128, width), 0),
                    (((1,), (1,)), ((), ())),
                    preferred_element_type=jnp.float32,
                )
            return 0

        lax.fori_loop(0, (n + group - 1) // group, one_group, 0)
        return 0

    lax.fori_loop(0, tiles, tile_step, 0)
    if last:
        for tile in range(tiles):
            outs[tile][...] = total[tile]
    else:
        outs[0][...] = total[...]


def stack_call(orders, slots, pieces, sources, before, tiles, with_fold, last):
    first = before is None
    sizes = tuple(piece.shape[0] for piece in pieces)
    rows = QUARTER + (FOLD if with_fold else 0)
    extra = [] if first else [before]
    whole = jax.ShapeDtypeStruct((tiles, rows, 256), jnp.float32)
    out_shape = [jax.ShapeDtypeStruct((rows, 256), jnp.float32)] * tiles if last else [whole]
    return pl.pallas_call(
        functools.partial(stack_kernel, (sizes, sources, tiles, with_fold, first, last)),
        out_shape=out_shape,
        in_specs=[IN_SMEM] * 4 + [IN_VMEM] + [IN_ANY] * len(pieces) + [IN_VMEM] * len(extra),
        out_specs=[IN_VMEM] * len(out_shape),
        scratch_shapes=[
            pltpu.VMEM((sum(sizes), 128), jnp.bfloat16),
            pltpu.VMEM(whole.shape, jnp.float32),
            pltpu.SMEM((256,), jnp.int32),
            pltpu.SemaphoreType.DMA((len(pieces),)),
        ],
        compiler_params=pltpu.CompilerParams(vmem_limit_bytes=32 * MIB),
        cost_estimate=pl.CostEstimate(
            flops=sources * tiles * 2 * 2 * QUARTER * 128 * 256,
            bytes_accessed=sum(sizes) * 256 + 4 * MIB,
            transcendentals=0,
        ),
        name="stack",
    )(*orders, *slots, *pieces, *extra)


def image_kernel(half, *refs):
    parts = refs[:4]
    if half == 0:
        packed, value_out, fold_out = refs[4:]
        fold = sum(part[QUARTER:] for part in parts)
        fold_out[...] = fold
    else:
        fold_in, before, packed, image = refs[4:]
        fold = fold_in[...]
    fold = jnp.maximum(fold, 1.0)
    left = low_lanes((CXL, 128))
    for a in range(CIL // 4):
        here = slice(a * CXL, (a + 1) * CXL)
        columns = []
        for q in range(4):
            lane = q * (CIL // 4) + a
            columns.append(
                jnp.concatenate(
                    [fold[:, 32 * j + lane : 32 * j + lane + 1] for j in range(3)], axis=0
                )
            )
        for side in range(2):
            lanes = slice(128 * side, 128 * side + 128)
            total = (parts[0][here, lanes] + parts[1][here, lanes]) + (
                parts[2][here, lanes] + parts[3][here, lanes]
            )
            value = total / jnp.where(left, columns[2 * side], columns[2 * side + 1])
            packed[here, lanes] = value.astype(jnp.bfloat16)
            if half == 0:
                value_out[here, lanes] = value
            else:
                earlier = before[here, lanes]
                even, odd = 2 * side * QUARTER + a * CXL, (2 * side + 1) * QUARTER + a * CXL
                image[even : even + CXL] = jnp.where(left, earlier, swap_lanes(value))
                image[odd : odd + CXL] = jnp.where(left, swap_lanes(earlier), value)


def image_call(half, parts, extra):
    packed = jax.ShapeDtypeStruct((QUARTER, 256), jnp.bfloat16)
    if half == 0:
        out_shape = [
            packed,
            jax.ShapeDtypeStruct((QUARTER, 256), jnp.float32),
            jax.ShapeDtypeStruct((FOLD, 256), jnp.float32),
        ]
    else:
        out_shape = [packed, jax.ShapeDtypeStruct((CELLS, 128), jnp.float32)]
    return pl.pallas_call(
        functools.partial(image_kernel, half),
        out_shape=out_shape,
        in_specs=[IN_VMEM] * (len(parts) + len(extra)),
        out_specs=[IN_VMEM] * len(out_shape),
        name=f"image_{half}",
    )(*parts, *extra)


def read_kernel(spec, order, counts, blocks, cells, own, *refs):
    sizes, half, first, last = spec
    group = 4
    tiles = sum(sizes) // QUARTER
    pieces = refs[: len(sizes)]
    refs = refs[len(sizes) :]
    if last:
        matrices, refs = refs[0], refs[1:]
    if not first:
        before, refs = refs[0], refs[1:]
    out, held, mine, total, sems = refs
    copies = [pltpu.make_async_copy(own, mine, sems.at[0])]
    start = 0
    for i, rows in enumerate(sizes):
        copies.append(
            pltpu.make_async_copy(pieces[i], held.at[pl.ds(start, rows)], sems.at[i + 1])
        )
        start += rows
    for copy in copies:
        copy.start()
    total[...] = jnp.zeros_like(total) if first else before[...]
    for copy in copies:
        copy.wait()
    left = low_lanes((128, 128))
    inside = left if half == 0 else jnp.logical_not(left)

    def tile_step(j, unused):
        tile = order[j]
        n = counts[tile]
        rows = cells[pl.ds(pl.multiple_of(tile * 8, 8), 8), :]
        quarters = quarter_of(rows)
        columns = (rows - QUARTER * quarters).T
        spots = quarters.T
        image = held[pl.ds(pl.multiple_of(j * QUARTER, QUARTER), QUARTER), :]
        for g in range(8 // group):

            @pl.when(n > g * group)
            def _():
                picks = [columns[:, g * group + i : g * group + i + 1] for i in range(group)]
                selector = jnp.concatenate(
                    [hot(pick, (128, QUARTER), 1) for pick in picks], axis=0
                )
                got = jnp.dot(selector, image, preferred_element_type=jnp.float32)
                for i, pick in enumerate(picks):
                    start = blocks[tile * 8 + g * group + i] * 128
                    here = pl.ds(pl.multiple_of(start, 128), 128)
                    spot = spots[:, g * group + i : g * group + i + 1]
                    part = got[i * 128 : (i + 1) * 128]
                    value = jnp.where(spot >= 2, part[:, 128:], part[:, :128])
                    stay = (spot & 1) == half
                    value = jnp.where(stay, value, swap_lanes(value))
                    sent = jnp.where(pick >= 0, mine[here, :].astype(jnp.float32), 0.0)
                    total[here, :] += jnp.where(inside, sent - value, 0.0)

        return 0

    lax.fori_loop(0, tiles, tile_step, 0)
    if not last:
        out[...] = total[...]
        return
    surveys = matrices.shape[0]
    rows = total.shape[0] // surveys
    sends = []
    for survey in range(surveys):
        here = slice(survey * rows, (survey + 1) * rows)
        total[here] = lax.dot_general(
            total[here].astype(jnp.bfloat16),
            matrices[survey],
            (((1,), (1,)), ((), ())),
            preferred_element_type=jnp.float32,
        )
        sends.append(
            pltpu.make_async_copy(
                total.at[pl.ds(survey * rows, rows)],
                out.at[pl.ds(survey * rows, rows)],
                sems.at[len(sizes) + 1 + survey],
            )
        )
        sends[-1].start()
    for send in sends:
        send.wait()


def read_call(half, order, slots, own, pieces, before, matrices=None):
    first, last = before is None, matrices is not None
    sizes = tuple(piece.shape[0] for piece in pieces)
    extra = ([matrices] if last else []) + ([] if first else [before])
    surveys = matrices.shape[0] if last else 0
    tiles = sum(sizes) // QUARTER
    return pl.pallas_call(
        functools.partial(read_kernel, (sizes, half, first, last)),
        out_shape=jax.ShapeDtypeStruct(own.shape, jnp.float32),
        in_specs=[IN_SMEM] * 3
        + [IN_VMEM]
        + [IN_ANY] * (1 + len(pieces))
        + [IN_VMEM] * len(extra),
        out_specs=IN_ANY if last else IN_VMEM,
        scratch_shapes=[
            pltpu.VMEM((sum(sizes), 256), jnp.bfloat16),
            pltpu.VMEM(own.shape, jnp.bfloat16),
            pltpu.VMEM(own.shape, jnp.float32),
            pltpu.SemaphoreType.DMA((len(sizes) + 1 + surveys,)),
        ],
        compiler_params=pltpu.CompilerParams(vmem_limit_bytes=32 * MIB),
        cost_estimate=pl.CostEstimate(
            flops=tiles * 4 * 2 * QUARTER * 128 * 256,
            bytes_accessed=8 * MIB,
            transcendentals=0,
        ),
        name="read",
    )(order, *slots, own, *pieces, *extra)


def with_halo(block, sides, width):
    for axis, count, dim in sides:
        forward = [(i, i + 1) for i in range(count - 1)]
        backward = [(target, source) for source, target in forward]
        low = lax.ppermute(
            lax.slice_in_dim(block, block.shape[dim] - width, None, axis=dim), axis, forward
        )
        high = lax.ppermute(lax.slice_in_dim(block, 0, width, axis=dim), axis, backward)
        block = jnp.concatenate([low, block, high], axis=dim)
    return block


def cycle_box(values, rows_out, cols_out):
    box_total = jnp.zeros((rows_out, cols_out, values.shape[2]), jnp.float32)
    for row_shift in range(3):
        for col_shift in range(3):
            box_total = (
                box_total
                + values[row_shift : row_shift + rows_out, col_shift : col_shift + cols_out]
            )
    return box_total / 9.0


def tensor(tile_image, il, xl):
    axis_il, count_il, at_il = il
    axis_xl, count_xl, at_xl = xl
    padded = with_halo(tile_image, ((axis_il, count_il, 0), (axis_xl, count_xl, 1)), 2)
    padded_time = jnp.pad(padded, ((0, 0), (0, 0), (1, 1)))
    grad_il = (padded[2:, 1:-1] - padded[:-2, 1:-1]) * 0.5
    grad_xl = (padded[1:-1, 2:] - padded[1:-1, :-2]) * 0.5
    grad_time = (padded_time[1:-1, 1:-1, 2:] - padded_time[1:-1, 1:-1, :-2]) * 0.5
    rows_il = at_il * CIL + jnp.arange(CIL + 2, dtype=jnp.int32) - 1
    rows_xl = at_xl * CXL + jnp.arange(CXL + 2, dtype=jnp.int32) - 1
    inside_il = ((rows_il >= 0) & (rows_il < CIL * count_il)).astype(jnp.float32)
    inside_xl = ((rows_xl >= 0) & (rows_xl < CXL * count_xl)).astype(jnp.float32)
    cycle_mask = inside_il[:, None, None] * inside_xl[None, :, None]
    factor_pairs = (
        (grad_il, grad_il),
        (grad_xl, grad_xl),
        (grad_time, grad_time),
        (grad_il, grad_xl),
        (grad_il, grad_time),
        (grad_xl, grad_time),
    )
    return jnp.stack(
        [
            cycle_box(left_part * right_part * cycle_mask, CIL, CXL)
            for left_part, right_part in factor_pairs
        ]
    )


SWAP = [(0, 1), (1, 0)]


def over(axis, value):
    return lax.ppermute(value, axis, SWAP)


def along_z(value, step):
    return lax.ppermute(value, "z", [(i, (i + step) % 4) for i in range(4)])


def local_planes(traces, filter_taps, slot_block, slot_cells, pair_count):
    row_block = slot_cells.shape[3]
    capacity = slot_block.shape[2]
    samples = traces.shape[1]
    surveys, tap_count = filter_taps.shape
    x, core, z, y = (lax.axis_index(name) for name in ("x", "c", "z", "y"))
    other = 1 - core

    slot_live = jnp.arange(capacity, dtype=jnp.int32)[None, :] < pair_count[0][:, None]
    out_cells = jnp.where(slot_live[:, :, None], slot_cells[0], -1)
    numbers = jnp.concatenate([slot_block[0], pair_count[0][:, None]], axis=1)
    numbers = jnp.pad(numbers, ((0, 0), (0, row_block - 8)))
    slots = jnp.concatenate([out_cells, numbers[:, None, :]], axis=1)
    by_column = slots.reshape(2, 2, 4, 2, 8, row_block).transpose(0, 1, 3, 2, 4, 5)
    arrived = lax.all_to_all(
        by_column.reshape(8, 4, 8, row_block), ("x", "c", "y"), 0, 0, tiled=True
    )
    in_numbers = arrived[:, :, 7, :8].reshape(32, 8)
    in_slots = (in_numbers[:, 7], in_numbers.reshape(256), arrived.reshape(256, row_block))
    own_cells = jnp.pad(out_cells, ((0, 0), (0, 1), (0, 0)), constant_values=-1)
    own_slots = (pair_count[0], numbers[:, :8].reshape(256), own_cells.reshape(256, row_block))

    taps = jnp.pad(filter_taps, ((0, 0), (0, samples - tap_count))).reshape(surveys, 1, samples)
    rows_half = traces.shape[0] // 2
    first_half, matrices = filter_call(0, traces, taps)
    second_half, filtered = filter_call(1, traces, taps)
    filtered = filtered.reshape(traces.shape)

    def column(*sources):
        return jnp.stack([(at_x * 2 + at_core) * 2 + at_y for at_x, at_core, at_y in sources])

    def tile_at(at_x, at_core, step, at_y):
        return ((at_x * 2 + at_core) * 4 + lax.rem(z + 4 - step, 4)) * 2 + at_y

    tile_order = jnp.stack([lax.rem(z + step, 4) for step in range(4)])
    near = column(
        (x, core, y),
        (x, other, y),
        (1 - x, core, y),
        (1 - x, other, y),
        (x, core, 1 - y),
        (x, other, 1 - y),
    )
    far = column((1 - x, core, 1 - y), (1 - x, other, 1 - y))

    def spread(value):
        middle = value.shape[0] // 2
        from_x, from_y = over("x", value), over("y", value)
        return from_x, from_y, over("y", from_x[:middle]), over("x", from_y[middle:])

    residual = None
    ready = None
    stacked = None
    gathered = []
    for half, packed in enumerate((first_half, second_half)):
        packed = packed.reshape(rows_half, samples)
        if half == 1:
            packed = tie(packed, ready)
        from_x, from_y, part0, part1 = spread(packed)
        pieces = []
        for piece in (packed, from_x, from_y):
            pieces += [piece, over("c", piece)]
        (ready,) = stack_call((tile_order, near), in_slots, pieces, 6, None, 4, half == 0, False)
        part0, part1 = tie(part0, ready), tie(part1, ready)
        pieces = [part0, part1, over("c", part0), over("c", part1)]
        partial = stack_call((tile_order, far), in_slots, pieces, 2, ready, 4, half == 0, True)
        totals = [partial[0]] + [along_z(partial[step], step) for step in (2, 1, 3)]
        if half == 0:
            packed_image, stacked, fold = image_call(0, totals, [])
        else:
            packed_image, image = image_call(1, totals, [fold, stacked])
        layers = [packed_image] + [along_z(packed_image, step) for step in (1, 2, 3)]
        layers = jnp.concatenate(layers, axis=0)
        gathered.append((layers,) + spread(layers))

    structure_tensor = tensor(
        image.reshape(CIL, CXL, samples),
        (("x", "c"), 4, x * 2 + core),
        (("z", "y"), 8, z * 2 + y),
    )

    spots = (
        (x, y, (0, 1, 2, 3)),
        (1 - x, y, (0, 1, 2, 3)),
        (x, 1 - y, (0, 1, 2, 3)),
        (1 - x, 1 - y, (0, 1)),
        (1 - x, 1 - y, (2, 3)),
    )

    def read(half, parts, before, last=None):
        pieces, order = [], []
        for part in parts:
            at_x, at_y, steps = spots[part]
            piece = gathered[half][part]
            if half == 1 and part >= 3:
                piece = tie(piece, before)
            pieces += [piece, over("c", piece)]
            order += [tile_at(at_x, core, step, at_y) for step in steps]
            order += [tile_at(at_x, other, step, at_y) for step in steps]
        return read_call(
            half, jnp.stack(order), own_slots, filtered, pieces, before, last
        )

    residual = read(0, (0, 1, 2, 3, 4), None)
    residual = read(1, (0,), residual)
    residual = read(1, (1, 2), residual)
    adjoint_traces = read(1, (3, 4), residual, matrices)
    return (structure_tensor, adjoint_traces)


def filter_matrices(filter_taps, samples):
    lag_table = (
        jnp.arange(samples, dtype=jnp.int32)[None, :]
        - jnp.arange(samples, dtype=jnp.int32)[:, None]
    )
    tap_count = filter_taps.shape[1]
    inside = (lag_table >= 0) & (lag_table < tap_count)
    picked = filter_taps[:, jnp.clip(lag_table, 0, tap_count - 1)]
    return jnp.where(inside[None], picked, 0.0).astype(jnp.bfloat16)


def local(traces, filter_taps, slot_block, slot_cells, pair_count):
    count_il = lax.axis_size("il")
    count_xl = lax.axis_size("xl")
    devices = count_il * count_xl
    samples = traces.shape[1]
    row_block = slot_cells.shape[3]
    capacity = slot_block.shape[2]
    surveys = filter_taps.shape[0]
    blocks_here = traces.shape[0] // row_block
    cell_count = CIL * CXL
    group_size = 16
    slot_total = devices * capacity
    group_count = slot_total // group_size
    matrices = filter_matrices(filter_taps, samples)
    by_survey = traces.reshape(surveys, blocks_here // surveys * row_block, samples)
    filtered = jnp.einsum("sru,sut->srt", by_survey, matrices, preferred_element_type=jnp.float32)
    filtered = filtered.astype(jnp.bfloat16).reshape(blocks_here, row_block, samples)
    block_ids = slot_block[0].reshape(-1)
    outgoing = jnp.take(filtered, block_ids, axis=0).reshape(devices, capacity, row_block, samples)
    slot_live = jnp.arange(capacity, dtype=jnp.int32)[None, :] < pair_count[0][:, None]
    out_cells = jnp.where(slot_live[:, :, None], slot_cells[0], -1)
    incoming, in_cells = (
        lax.all_to_all(outgoing, ("il", "xl"), split_axis=0, concat_axis=0, tiled=True),
        lax.all_to_all(out_cells, ("il", "xl"), split_axis=0, concat_axis=0, tiled=True),
    )
    incoming = incoming.reshape(slot_total, row_block, samples)
    in_cells = in_cells.reshape(slot_total, row_block)
    cell_line = jnp.arange(cell_count, dtype=jnp.int32)

    def one_hot(group_cells):
        return (cell_line[:, None] == group_cells.reshape(1, -1)).astype(jnp.bfloat16)

    def add_group(running, group_blocks, group_cells):
        stacked, fold_counts = running
        selector = one_hot(group_cells)
        stacked = stacked + jnp.dot(
            selector, group_blocks.reshape(-1, samples), preferred_element_type=jnp.float32
        )
        fold_counts = fold_counts + jnp.sum(selector, axis=1, dtype=jnp.float32)
        return (stacked, fold_counts)

    initial = (jnp.zeros((cell_count, samples), jnp.float32), jnp.zeros((cell_count,), jnp.float32))

    def scan_step(running, scan_item):
        return (add_group(running, scan_item[0], scan_item[1]), None)

    (stacked, fold_counts), unused = lax.scan(
        scan_step,
        initial,
        (
            incoming.reshape(group_count, group_size, row_block, samples),
            in_cells.reshape(group_count, group_size, row_block),
        ),
    )
    stack_image = stacked / jnp.maximum(fold_counts, 1.0)[:, None]
    image_half = stack_image.astype(jnp.bfloat16)

    def read_group(group_cells):
        selector = one_hot(group_cells)
        picked = lax.dot_general(
            selector, image_half, (((0,), (0,)), ((), ())), preferred_element_type=jnp.float32
        )
        return picked.astype(jnp.bfloat16).reshape(group_size, row_block, samples)

    answer = lax.map(read_group, in_cells.reshape(group_count, group_size, row_block)).reshape(
        slot_total, row_block, samples
    )
    returned = lax.all_to_all(
        answer.reshape(devices, capacity, row_block, samples),
        ("il", "xl"),
        split_axis=0,
        concat_axis=0,
        tiled=True,
    )
    returned = returned.reshape(slot_total, row_block, samples)
    out_valid = (out_cells >= 0).reshape(slot_total, row_block, 1)
    zero_half = jnp.zeros((), jnp.bfloat16)
    sent_part = jnp.where(out_valid, outgoing.reshape(slot_total, row_block, samples), zero_half)
    back_part = jnp.where(out_valid, returned, zero_half)
    selector_rows = (
        block_ids[:, None] == jnp.arange(blocks_here, dtype=jnp.int32)[None, :]
    ).astype(jnp.bfloat16)
    residual = jnp.einsum(
        "sb,sit->bit", selector_rows, sent_part, preferred_element_type=jnp.float32
    )
    residual = residual - jnp.einsum(
        "sb,sit->bit", selector_rows, back_part, preferred_element_type=jnp.float32
    )
    residual_half = residual.astype(jnp.bfloat16).reshape(surveys, -1, samples)
    adjoint_traces = jnp.einsum(
        "srt,sut->sru", residual_half, matrices, preferred_element_type=jnp.float32
    ).reshape(traces.shape)
    structure_tensor = tensor(
        stack_image.reshape(CIL, CXL, samples),
        ("il", count_il, lax.axis_index("il")),
        ("xl", count_xl, lax.axis_index("xl")),
    )
    return (structure_tensor, adjoint_traces)


def solution(mesh):
    inner, names, body = mesh, (("il",), ("xl",)), local
    if mesh.devices.shape == (4, 8):
        inner = Mesh(mesh.devices.reshape(2, 2, 4, 2), ("x", "c", "z", "y"))
        names, body = (("x", "c"), ("z", "y")), local_planes
    il, xl = names
    both = il + xl
    return jax.shard_map(
        body,
        mesh=inner,
        in_specs=(
            P(both, None),
            P(),
            P(both, None, None),
            P(both, None, None, None),
            P(both, None),
        ),
        out_specs=(P(None, il, xl, None), P(both, None)),
        check_vma=False,
    )
```

```python
import functools

import jax
import jax.numpy as jnp
from jax import lax
from jax.experimental import pallas as pl
from jax.experimental.pallas import tpu as pltpu
from jax.sharding import Mesh
from jax.sharding import PartitionSpec as P

CIL = 32
CXL = 48
CELLS = CIL * CXL
QUARTER = CELLS // 4
FOLD = CXL // 3
MIB = 1 << 20
VMEM_LIMIT = 56 * MIB
IN_SMEM = pl.BlockSpec(memory_space=pltpu.SMEM)
IN_VMEM = pl.BlockSpec(memory_space=pltpu.VMEM)
IN_ANY = pl.BlockSpec(memory_space=pl.ANY)
IN_HBM = pl.BlockSpec(memory_space=pltpu.HBM)

WEIGHT = pl.CostEstimate(flops=1 << 35, bytes_accessed=1 << 20, transcendentals=0)
LIGHT = pl.CostEstimate(flops=1, bytes_accessed=1, transcendentals=0)


def hot(cells, shape, axis):
    line = lax.broadcasted_iota(jnp.int32, shape, axis)
    return jnp.where(line == cells, 1.0, 0.0).astype(jnp.bfloat16)


def quarter_of(cells):
    return sum((cells >= q * QUARTER).astype(jnp.int32) for q in (1, 2, 3))


def low_lanes(shape):
    return lax.broadcasted_iota(jnp.int32, shape, len(shape) - 1) < 64


def swap_lanes(value):
    return pltpu.roll(value, 64, 1)


def tie(values, *tokens):
    count = len(values)

    def kernel(*refs):
        pass

    return pl.pallas_call(
        kernel,
        out_shape=[jax.ShapeDtypeStruct(value.shape, value.dtype) for value in values],
        in_specs=[IN_ANY] * (count + len(tokens)),
        out_specs=[IN_ANY] * count,
        input_output_aliases={i: i for i in range(count)},
        cost_estimate=LIGHT,
        name="tie",
    )(*values, *tokens)


def gate_kernel(skip, from_x, from_y, *refs):
    turn_x, turn_y, held, sems = refs[skip + 2 :]
    middle = turn_x.shape[0]
    copies = [
        pltpu.make_async_copy(from_x.at[pl.ds(0, middle)], held.at[0], sems.at[0]),
        pltpu.make_async_copy(from_y.at[pl.ds(middle, middle)], held.at[1], sems.at[1]),
    ]
    sends = [
        pltpu.make_async_copy(held.at[0], turn_x, sems.at[2]),
        pltpu.make_async_copy(held.at[1], turn_y, sems.at[3]),
    ]
    for copy in copies:
        copy.start()
    for copy, send in zip(copies, sends, strict=True):
        copy.wait()
        send.start()
    for send in sends:
        send.wait()


def gate(from_x, from_y, *tokens):
    full = jax.ShapeDtypeStruct(from_x.shape, from_x.dtype)
    part = jax.ShapeDtypeStruct((from_x.shape[0] // 2, from_x.shape[1]), from_x.dtype)
    return pl.pallas_call(
        functools.partial(gate_kernel, len(tokens)),
        out_shape=[full, full, part, part],
        in_specs=[IN_HBM] * 2 + [IN_ANY] * len(tokens),
        out_specs=[IN_HBM] * 4,
        input_output_aliases={0: 0, 1: 1},
        scratch_shapes=[
            pltpu.VMEM((2,) + part.shape, part.dtype),
            pltpu.SemaphoreType.DMA((4,)),
        ],
        name="gate",
    )(from_x, from_y, *tokens)


def filter_kernel(half, skip, taps, source, *refs):
    out, *matrices = refs[skip:]
    each, rows, samples = source.shape
    row = lax.broadcasted_iota(jnp.int32, (samples, samples), 0)
    col = lax.broadcasted_iota(jnp.int32, (samples, samples), 1)
    for i in range(each):
        line = jnp.broadcast_to(taps[i], (samples, samples))
        band = pltpu.roll(line, 0, 1, stride=1, stride_axis=0)
        matrix = jnp.where(col >= row, band, 0.0)
        if matrices:
            matrices[0][i] = matrix.astype(jnp.bfloat16)
        turned = matrix.T[64 * half : 64 * half + 64].astype(jnp.bfloat16)
        value = lax.dot_general(
            turned, source[i], (((1,), (1,)), ((), ())), preferred_element_type=jnp.float32
        ).astype(jnp.bfloat16)
        for block in range(rows // 128):
            out[i, 64 * block : 64 * block + 64] = value[:, 128 * block : 128 * block + 128]


def filter_call(half, traces, taps, tokens=()):
    surveys, unused, samples = taps.shape
    rows = traces.shape[0] // surveys
    each = 3
    out_specs = [pl.BlockSpec((each, rows // 2, samples), lambda i: (i, 0, 0))]
    out_shape = [jax.ShapeDtypeStruct((surveys, rows // 2, samples), jnp.bfloat16)]
    if half == 1:
        out_specs.append(pl.BlockSpec((each, samples, samples), lambda i: (i, 0, 0)))
        out_shape.append(jax.ShapeDtypeStruct((surveys, samples, samples), jnp.bfloat16))
    return pl.pallas_call(
        functools.partial(filter_kernel, half, len(tokens)),
        grid=(surveys // each,),
        in_specs=[
            pl.BlockSpec((each, 1, samples), lambda i: (i, 0, 0)),
            pl.BlockSpec((each, rows, samples), lambda i: (i, 0, 0)),
        ]
        + [IN_ANY] * len(tokens),
        out_specs=out_specs,
        out_shape=out_shape,
        name=f"filter_{half}",
    )(taps, traces.reshape(surveys, rows, samples), *tokens)


def stack_kernel(spec, order, cells, *refs):
    sizes, sources, tiles, with_fold, first, last, skip, base = spec
    per_slot = cells.shape[1]
    group = 16
    pieces = refs[: len(sizes)]
    refs = refs[len(sizes) :]
    if not first:
        before, refs = refs[0], refs[1:]
    refs = refs[skip:]
    outs = refs[: tiles if last else 1]
    held, total, live, numbers, sems = refs[len(outs) :]
    copies = []
    start = 0
    for i, rows in enumerate(sizes):
        copies.append(
            pltpu.make_async_copy(pieces[i], held.at[pl.ds(start, rows)], sems.at[i])
        )
        start += rows
    per_source = start // sources
    if not first:
        copies.append(pltpu.make_async_copy(before, total, sems.at[len(sizes)]))
    origins = cells.shape[0]
    for i in range(origins):
        copies.append(
            pltpu.make_async_copy(
                cells.at[i, pl.ds(per_slot - 8, 8)],
                numbers.at[pl.ds(8 * i, 8)],
                sems.at[len(sizes) + 1 + tiles + i],
            )
        )
    for copy in copies:
        copy.start()
    if first:
        total[...] = jnp.zeros_like(total)
    for copy in copies:
        copy.wait()

    def tile_step(tile, unused):
        def add_source(source, n):
            origin = order[base + source]
            wanted = order[tile]

            def add_slot(c, n):
                live[n] = wanted * 8 + c
                live[n + 128] = numbers[origin * 8 + wanted, c] * 64 + source * per_source
                live[n + 256] = origin
                return n + 1

            return lax.fori_loop(0, numbers[origin * 8 + wanted, 7], add_slot, n)

        n = lax.fori_loop(0, sources, add_source, 0)

        def one_group(g, unused):
            picked, data, selector = [], [], []
            for i in range(group):
                at = g * group + i
                place = jnp.minimum(at, n - 1)
                row = jnp.where(at < n, cells[live[256 + place], pl.ds(live[place], 1), :], -1)
                quarter = quarter_of(row)
                block = held[pl.ds(pl.multiple_of(live[128 + place], 64), 64), :]
                block = block.astype(jnp.float32)
                data.append(
                    jnp.concatenate(
                        [jnp.where(quarter == q, block, 0.0) for q in range(4)], axis=0
                    ).astype(jnp.bfloat16)
                )
                selector.append(hot(row - QUARTER * quarter, (QUARTER, 128), 0))
                picked.append(row)
            total[tile, :QUARTER] += lax.dot_general(
                jnp.concatenate(selector, axis=1),
                jnp.concatenate(data, axis=1),
                (((1,), (1,)), ((), ())),
                preferred_element_type=jnp.float32,
            )
            line = jnp.concatenate(picked, axis=1)
            width = line.shape[1]
            if with_fold:
                inline = ((line >> 4) * 171) >> 9
                cross = line - CXL * inline
                row = jnp.where(line >= 0, cross & 15, -1)
                lane = inline + 32 * (cross >> 4)
                total[tile, QUARTER:, :128] += lax.dot_general(
                    hot(row, (FOLD, width), 0),
                    hot(lane, (128, width), 0),
                    (((1,), (1,)), ((), ())),
                    preferred_element_type=jnp.float32,
                )
            return 0

        lax.fori_loop(0, (n + group - 1) // group, one_group, 0)
        return 0

    lax.fori_loop(0, tiles, tile_step, 0)
    targets = [total.at[tile] for tile in range(tiles)] if last else [total]
    sends = [
        pltpu.make_async_copy(target, out, sems.at[len(sizes) + 1 + i])
        for i, (target, out) in enumerate(zip(targets, outs, strict=True))
    ]
    for send in sends:
        send.start()
    for send in sends:
        send.wait()


def stack_call(order, base, cells, pieces, sources, before, tiles, with_fold, last, tokens=()):
    first = before is None
    sizes = tuple(piece.shape[0] for piece in pieces)
    rows = QUARTER + (FOLD if with_fold else 0)
    extra = [] if first else [before]
    every = jax.ShapeDtypeStruct((tiles, rows, 256), jnp.float32)
    single = [jax.ShapeDtypeStruct((rows, 256), jnp.float32)] * tiles
    origins = cells.shape[0]
    spec = (sizes, sources, tiles, with_fold, first, last, len(tokens), base)
    return pl.pallas_call(
        functools.partial(stack_kernel, spec),
        out_shape=single if last else [every],
        in_specs=[IN_SMEM, IN_VMEM]
        + [IN_HBM] * (len(pieces) + len(extra))
        + [IN_ANY] * len(tokens),
        out_specs=[IN_HBM] * (tiles if last else 1),
        scratch_shapes=[
            pltpu.VMEM((sum(sizes), 128), jnp.bfloat16),
            pltpu.VMEM(every.shape, jnp.float32),
            pltpu.SMEM((384,), jnp.int32),
            pltpu.SMEM((8 * origins, 128), jnp.int32),
            pltpu.SemaphoreType.DMA((len(pieces) + 1 + tiles + origins,)),
        ],
        compiler_params=pltpu.CompilerParams(vmem_limit_bytes=VMEM_LIMIT),
        cost_estimate=LIGHT if last else WEIGHT,
        name="stack",
    )(order, cells, *pieces, *extra, *tokens)


def image_kernel(half, skip, *refs):
    parts, refs = refs[:4], refs[4:]
    if half == 0:
        packed, value_out, fold_out, turned = refs[skip:]
        fold = sum(parts[i][QUARTER:] for i in range(4))
        fold_out[...] = fold
    else:
        fold_in, before, packed, image, turned = refs[:2] + refs[2 + skip :]
        fold = fold_in[...]
    fold = jnp.maximum(fold, 1.0)
    left = low_lanes((CXL, 128))
    for a in range(CIL // 4):
        here = slice(a * CXL, (a + 1) * CXL)
        columns = []
        for q in range(4):
            lane = q * (CIL // 4) + a
            columns.append(
                jnp.concatenate(
                    [fold[:, 32 * j + lane : 32 * j + lane + 1] for j in range(3)], axis=0
                )
            )
        for side in range(2):
            lanes = slice(128 * side, 128 * side + 128)
            total = (parts[0][here, lanes] + parts[1][here, lanes]) + (
                parts[2][here, lanes] + parts[3][here, lanes]
            )
            value = total / jnp.where(left, columns[2 * side], columns[2 * side + 1])
            turned[here, lanes] = value
            if half == 0:
                value_out[here, lanes] = value
            else:
                earlier = before[here, lanes]
                even, odd = 2 * side * QUARTER + a * CXL, (2 * side + 1) * QUARTER + a * CXL
                image[even : even + CXL] = jnp.where(left, earlier, swap_lanes(value))
                image[odd : odd + CXL] = jnp.where(left, swap_lanes(earlier), value)
    copy = turned[...].T.astype(jnp.bfloat16)
    for i in range(4):
        packed[256 * i : 256 * i + 256] = copy


def image_call(half, parts, extra, tokens):
    packed = jax.ShapeDtypeStruct((4 * 256, QUARTER), jnp.bfloat16)
    if half == 0:
        out_shape = [
            packed,
            jax.ShapeDtypeStruct((QUARTER, 256), jnp.float32),
            jax.ShapeDtypeStruct((FOLD, 256), jnp.float32),
        ]
    else:
        out_shape = [packed, jax.ShapeDtypeStruct((CELLS, 128), jnp.float32)]
    return pl.pallas_call(
        functools.partial(image_kernel, half, len(tokens)),
        out_shape=out_shape,
        in_specs=[IN_VMEM] * (4 + len(extra)) + [IN_ANY] * len(tokens),
        out_specs=[IN_VMEM] * len(out_shape),
        scratch_shapes=[pltpu.VMEM((QUARTER, 256), jnp.float32)],
        cost_estimate=LIGHT,
        name=f"image_{half}",
    )(*parts, *extra, *tokens)


def read_kernel(spec, order, counts, blocks, cells, own, *refs):
    sizes, first, last, skip, base = spec
    group = 4
    tiles = sum(sizes) // 256
    pieces = refs[: len(sizes)]
    refs = refs[len(sizes) :]
    if last:
        matrices, earlier, refs = refs[0], refs[1], refs[2:]
    if not first:
        before, refs = refs[0], refs[1:]
    refs = refs[skip:]
    out, held, mine, total, live, sems = refs[:6]
    copies = [pltpu.make_async_copy(own, mine, sems.at[0])]
    if not first:
        copies.append(pltpu.make_async_copy(before, total, sems.at[len(sizes) + 1]))
    if last:
        whole_out, earlier_in, band = refs[6:]
        copies.append(pltpu.make_async_copy(earlier, earlier_in, sems.at[len(sizes) + 2]))
        copies.append(pltpu.make_async_copy(matrices, band, sems.at[len(sizes) + 3]))
    start = 0
    for i, rows in enumerate(sizes):
        copies.append(
            pltpu.make_async_copy(pieces[i], held.at[pl.ds(start, rows)], sems.at[i + 1])
        )
        start += rows
    for copy in copies:
        copy.start()
    if first:
        total[...] = jnp.zeros_like(total)

    def add_tile(j, n):
        for g in range(8 // group):
            live[n] = order[base + j] * 8 + g * group
            live[n + 128] = j
            n = n + (counts[order[base + j]] > g * group).astype(jnp.int32)
        return n

    n = lax.fori_loop(0, tiles, add_tile, 0)
    for copy in copies:
        copy.wait()

    def one_step(step, unused):
        waiting = []
        for k in range(2):
            at = step * 2 + k
            place = jnp.minimum(at, n - 1)
            entry = live[place]
            rows = [
                jnp.where(at < n, cells[pl.ds(entry + i, 1), :], -1) for i in range(group)
            ]
            quarters = [quarter_of(row) for row in rows]
            selector = jnp.concatenate(
                [
                    hot(row - QUARTER * quarter, (QUARTER, 128), 0)
                    for row, quarter in zip(rows, quarters, strict=True)
                ],
                axis=1,
            )
            image = held[pl.ds(pl.multiple_of(live[128 + place] * 256, 256), 256), :]
            got = jnp.dot(image, selector, preferred_element_type=jnp.float32)
            waiting.append((entry, rows, quarters, got))
        for entry, rows, quarters, got in waiting:
            for i in range(group):
                here = pl.ds(pl.multiple_of(blocks[entry + i] * 64, 64), 64)
                part = got[:, 128 * i : 128 * i + 128]
                value = part[:64]
                for q in (1, 2, 3):
                    value = jnp.where(quarters[i] == q, part[64 * q : 64 * q + 64], value)
                sent = jnp.where(rows[i] >= 0, mine[here, :].astype(jnp.float32), 0.0)
                total[here, :] += sent - value
        return 0

    lax.fori_loop(0, (n + 1) // 2, one_step, 0)
    if not last:
        send = pltpu.make_async_copy(total, out, sems.at[len(sizes) + 4])
        send.start()
        send.wait()
        return
    surveys = matrices.shape[0]
    rows = whole_out.shape[0] // surveys
    sends = []
    for survey in range(surveys):
        for block in range(rows // 128):
            at = survey * (rows // 2) + block * 64
            residual = jnp.concatenate(
                [earlier_in[at : at + 64], total[at : at + 64]], axis=0
            ).T.astype(jnp.bfloat16)
            whole_out[survey * rows + 128 * block : survey * rows + 128 * block + 128] = (
                lax.dot_general(
                    residual,
                    band[survey],
                    (((1,), (1,)), ((), ())),
                    preferred_element_type=jnp.float32,
                )
            )
        sends.append(
            pltpu.make_async_copy(
                whole_out.at[pl.ds(survey * rows, rows)],
                out.at[pl.ds(survey * rows, rows)],
                sems.at[len(sizes) + 4 + survey],
            )
        )
        sends[-1].start()
    for send in sends:
        send.wait()


def read_call(
    order, base, slots, own, pieces, before, matrices=None, earlier=None, tokens=(), cost=None
):
    first, last = before is None, matrices is not None
    sizes = tuple(piece.shape[0] for piece in pieces)
    extra = ([matrices, earlier] if last else []) + ([] if first else [before])
    surveys = matrices.shape[0] if last else 0
    full = (2 * own.shape[0], own.shape[1])
    return pl.pallas_call(
        functools.partial(read_kernel, (sizes, first, last, len(tokens), base)),
        out_shape=jax.ShapeDtypeStruct(full if last else own.shape, jnp.float32),
        in_specs=[IN_SMEM] * 3
        + [IN_VMEM]
        + [IN_HBM] * (1 + len(pieces))
        + [IN_HBM] * len(extra)
        + [IN_ANY] * len(tokens),
        out_specs=IN_HBM,
        scratch_shapes=[
            pltpu.VMEM((sum(sizes), QUARTER), jnp.bfloat16),
            pltpu.VMEM(own.shape, jnp.bfloat16),
            pltpu.VMEM(own.shape, jnp.float32),
            pltpu.SMEM((256,), jnp.int32),
            pltpu.SemaphoreType.DMA((len(sizes) + 5 + surveys,)),
        ]
        + (
            [
                pltpu.VMEM(full, jnp.float32),
                pltpu.VMEM(own.shape, jnp.float32),
                pltpu.VMEM(matrices.shape, jnp.bfloat16),
            ]
            if last
            else []
        ),
        compiler_params=pltpu.CompilerParams(vmem_limit_bytes=VMEM_LIMIT),
        cost_estimate=cost or LIGHT,
        name="read",
    )(order, *slots, own, *pieces, *extra, *tokens)


def with_halo(block, sides, width):
    for axis, count, dim in sides:
        forward = [(i, i + 1) for i in range(count - 1)]
        backward = [(target, source) for source, target in forward]
        low = lax.ppermute(
            lax.slice_in_dim(block, block.shape[dim] - width, None, axis=dim), axis, forward
        )
        high = lax.ppermute(lax.slice_in_dim(block, 0, width, axis=dim), axis, backward)
        block = jnp.concatenate([low, block, high], axis=dim)
    return block


def cycle_box(values, rows_out, cols_out):
    box_total = jnp.zeros((rows_out, cols_out, values.shape[2]), jnp.float32)
    for row_shift in range(3):
        for col_shift in range(3):
            box_total = (
                box_total
                + values[row_shift : row_shift + rows_out, col_shift : col_shift + cols_out]
            )
    return box_total / 9.0


def tensor(padded, il, xl):
    count_il, at_il = il
    count_xl, at_xl = xl
    padded_time = jnp.pad(padded, ((0, 0), (0, 0), (1, 1)))
    grad_il = (padded[2:, 1:-1] - padded[:-2, 1:-1]) * 0.5
    grad_xl = (padded[1:-1, 2:] - padded[1:-1, :-2]) * 0.5
    grad_time = (padded_time[1:-1, 1:-1, 2:] - padded_time[1:-1, 1:-1, :-2]) * 0.5
    rows_il = at_il * CIL + jnp.arange(CIL + 2, dtype=jnp.int32) - 1
    rows_xl = at_xl * CXL + jnp.arange(CXL + 2, dtype=jnp.int32) - 1
    inside_il = ((rows_il >= 0) & (rows_il < CIL * count_il)).astype(jnp.float32)
    inside_xl = ((rows_xl >= 0) & (rows_xl < CXL * count_xl)).astype(jnp.float32)
    cycle_mask = inside_il[:, None, None] * inside_xl[None, :, None]
    factor_pairs = (
        (grad_il, grad_il),
        (grad_xl, grad_xl),
        (grad_time, grad_time),
        (grad_il, grad_xl),
        (grad_il, grad_time),
        (grad_xl, grad_time),
    )
    return jnp.stack(
        [
            cycle_box(left_part * right_part * cycle_mask, CIL, CXL)
            for left_part, right_part in factor_pairs
        ]
    )


def tensor_kernel(place, image, low_il, high_il, low_xl, high_xl, out, padded, boxed):
    padded[:2, 2 : CXL + 2] = low_il[...]
    padded[2 : CIL + 2, 2 : CXL + 2] = image[...]
    padded[CIL + 2 :, 2 : CXL + 2] = high_il[...]
    padded[:, :2] = low_xl[...]
    padded[:, CXL + 2 : CXL + 4] = high_xl[...]
    shape = (CXL + 2, 128)
    col = lax.broadcasted_iota(jnp.int32, shape, 0) + (place[2] * CXL - 1)
    lane = lax.broadcasted_iota(jnp.int32, shape, 1)
    inside = (col >= 0) & (col < CXL * place[3])

    def one_row(r, unused):
        row = place[0] * CIL + r - 1
        here = inside & (row >= 0) & (row < CIL * place[1])
        middle = padded[r + 1, 1 : CXL + 3]
        later = jnp.where(lane < 127, pltpu.roll(middle, 127, 1), 0.0)
        earlier = jnp.where(lane > 0, pltpu.roll(middle, 1, 1), 0.0)
        along = [
            (padded[r + 2, 1 : CXL + 3] - padded[r, 1 : CXL + 3]) * 0.5,
            (padded[r + 1, 2 : CXL + 4] - padded[r + 1, 0 : CXL + 2]) * 0.5,
            (later - earlier) * 0.5,
        ]
        along = [jnp.where(here, part, 0.0) for part in along]
        for k, (i, j) in enumerate(((0, 0), (1, 1), (2, 2), (0, 1), (0, 2), (1, 2))):
            product = along[i] * along[j]
            boxed[k, r] = (product[:CXL] + product[1 : CXL + 1]) + product[2:]
        return 0

    lax.fori_loop(0, CIL + 2, one_row, 0)

    def one_out(r, unused):
        for k in range(6):
            out[k, r] = ((boxed[k, r] + boxed[k, r + 1]) + boxed[k, r + 2]) / 9.0
        return 0

    lax.fori_loop(0, CIL, one_out, 0)


def tensor_call(place, image, halo, tokens=()):
    def kernel(*refs):
        tensor_kernel(*refs[:6], *refs[6 + len(tokens) :])

    return pl.pallas_call(
        kernel,
        out_shape=jax.ShapeDtypeStruct((6, CIL, CXL, 128), jnp.float32),
        in_specs=[IN_SMEM] + [IN_VMEM] * 5 + [IN_ANY] * len(tokens),
        out_specs=IN_VMEM,
        scratch_shapes=[
            pltpu.VMEM((CIL + 4, CXL + 8, 128), jnp.float32),
            pltpu.VMEM((6, CIL + 2, CXL, 128), jnp.float32),
        ],
        compiler_params=pltpu.CompilerParams(vmem_limit_bytes=VMEM_LIMIT),
        cost_estimate=LIGHT,
        name="tensor",
    )(place, image, *halo, *tokens)


def halo_of(image, side_il, side_xl):
    axis_il, count_il = side_il
    axis_xl, count_xl = side_xl
    up_il, up_xl = ([(i, i + 1) for i in range(n - 1)] for n in (count_il, count_xl))
    down_il, down_xl = ([(j, i) for i, j in up] for up in (up_il, up_xl))
    low_il = lax.ppermute(image[-2:], axis_il, up_il)
    high_il = lax.ppermute(image[:2], axis_il, down_il)

    def edge(cols):
        return jnp.concatenate([part[:, cols] for part in (low_il, image, high_il)], axis=0)

    low_xl = lax.ppermute(edge(slice(CXL - 2, CXL)), axis_xl, up_xl)
    high_xl = lax.ppermute(edge(slice(0, 2)), axis_xl, down_xl)
    return low_il, high_il, low_xl, high_xl


SWAP = [(0, 1), (1, 0)]


def along_z(value, step):
    return lax.ppermute(value, "z", [(i, (i + step) % 4) for i in range(4)])


def over(axis, value):
    return lax.ppermute(value, axis, SWAP)


def local_planes(traces, filter_taps, slot_block, slot_cells, pair_count):
    row_block = slot_cells.shape[3]
    capacity = slot_block.shape[2]
    samples = traces.shape[1]
    surveys, tap_count = filter_taps.shape
    x, core, z, y = (lax.axis_index(name) for name in ("x", "c", "z", "y"))
    other = 1 - core

    slot_live = jnp.arange(capacity, dtype=jnp.int32)[None, :] < pair_count[0][:, None]
    out_cells = jnp.where(slot_live[:, :, None], slot_cells[0], -1)
    own_cells = jnp.pad(out_cells, ((0, 0), (0, 1), (0, 0)), constant_values=-1)
    numbers = jnp.concatenate([slot_block[0], pair_count[0][:, None]], axis=1)

    def by_column(value):
        parts = value.reshape((2, 2, 4, 2) + value.shape[1:])
        return jnp.moveaxis(parts, 2, 3).reshape((8, 4) + value.shape[1:])

    arrived = lax.all_to_all(
        jnp.concatenate(
            [
                by_column(own_cells).reshape(8, 32, row_block),
                jnp.pad(by_column(numbers), ((0, 0), (0, 4), (0, row_block - 8))),
            ],
            axis=1,
        ),
        ("x", "c", "y"),
        0,
        0,
        tiled=True,
    )
    own_slots = (pair_count[0], numbers.reshape(256), own_cells.reshape(256, row_block))

    taps = jnp.pad(filter_taps, ((0, 0), (0, samples - tap_count))).reshape(surveys, 1, samples)
    rows_half = traces.shape[0] // 2
    (first_half,) = filter_call(0, traces, taps)
    second_half, matrices = filter_call(1, traces, taps)
    halves = [part.reshape(rows_half, samples) for part in (first_half, second_half)]

    spots = ((x, y), (1 - x, y), (x, 1 - y), (1 - x, 1 - y))
    orders = [lax.rem(z + step, 4) for step in range(4)]
    for at_x, at_y in spots:
        orders += [(at_x * 2 + at_core) * 2 + at_y for at_core in (core, other)]
    wanted = [(spot, core) for spot in spots[:3]] + [(spot, other) for spot in spots[:3]]
    wanted += [(spots[3], core), (spots[3], other)]
    wanted += [(spot, at_core) for spot in spots[:3] for at_core in (core, other)]
    for (at_x, at_y), at_core in wanted:
        orders += [((at_x * 2 + at_core) * 4 + at_z) * 2 + at_y for at_z in range(4)]
    orders = jnp.stack(orders)

    def spread(value, *tokens):
        from_x, from_y, turn_x, turn_y = gate(over("x", value), over("y", value), *tokens)
        return from_x, from_y, (over("y", turn_x), over("x", turn_y))

    def pairs(*pieces):
        return [part for piece in pieces for part in (piece, over("c", piece))]

    def near_stack(half, pieces, tokens=()):
        return stack_call(orders, 4, arrived, pieces, 6, None, 4, half == 0, False, tokens)[0]

    def far_stack(half, parts, before):
        pieces = [*parts, *(over("c", part) for part in parts)]
        return stack_call(orders, 10, arrived, pieces, 2, before, 4, half == 0, True)

    def sum_z(partial):
        return [partial[0]] + [along_z(partial[step], step) for step in (2, 1, 3)]

    def over_z(value):
        return lax.all_to_all(value, "z", 0, 0, tiled=True)

    def read(half, base, pieces, *rest, **named):
        return read_call(orders, base, own_slots, halves[half], pieces, *rest, **named)


    from_x, from_y, parts = spread(halves[0], halves[1], arrived, orders, *own_slots)
    near_0 = near_stack(0, pairs(halves[0], from_x, from_y))
    (own_1,) = tie([halves[1]], near_0)
    halves[1] = own_1
    partial_0 = far_stack(0, tie(parts, near_0), near_0)
    packed_0, stacked, fold = image_call(0, sum_z(partial_0), [], [])
    columns_0 = over_z(packed_0)
    from_x, from_y, parts = spread(own_1, packed_0)
    near_1 = near_stack(1, pairs(own_1, from_x, from_y))
    partial_1 = far_stack(1, tie(parts, near_1), near_1)
    from_x, from_y, parts = spread(columns_0, partial_1[0])
    own_layers = [columns_0, from_x, from_y]
    residual_0 = read(0, 12, own_layers, None)
    packed_1, image = image_call(1, sum_z(partial_1), [fold, stacked], [residual_0, *parts])
    columns_1 = over_z(packed_1)
    image = image.reshape(CIL, CXL, samples)
    halo = halo_of(image, (("x", "c"), 4), (("z", "y"), 8))
    place = jnp.stack([x * 2 + core, jnp.int32(4), z * 2 + y, jnp.int32(8)])
    own_layers = tie([*own_layers, *parts], packed_1)
    layers = [over("c", layer) for layer in own_layers]
    layers = layers[:3] + list(own_layers[3:]) + layers[3:]
    residual_0 = read(0, 24, layers, residual_0, tokens=[columns_1, *halo])
    structure_tensor = tensor_call(place, image, halo, [residual_0])
    residual_1 = read(1, 44, pairs(columns_1), None, tokens=[structure_tensor])
    from_x, from_y, parts = spread(columns_1, residual_1)
    residual_1 = read(1, 52, pairs(from_x, from_y), residual_1)
    parts = tie(parts, residual_1)
    layers = [*parts, *(over("c", part) for part in parts)]
    adjoint_traces = read(1, 36, layers, residual_1, matrices, residual_0)
    return (structure_tensor, adjoint_traces)


def filter_matrices(filter_taps, samples):
    lag_table = (
        jnp.arange(samples, dtype=jnp.int32)[None, :]
        - jnp.arange(samples, dtype=jnp.int32)[:, None]
    )
    tap_count = filter_taps.shape[1]
    inside = (lag_table >= 0) & (lag_table < tap_count)
    picked = filter_taps[:, jnp.clip(lag_table, 0, tap_count - 1)]
    return jnp.where(inside[None], picked, 0.0).astype(jnp.bfloat16)


def local(traces, filter_taps, slot_block, slot_cells, pair_count):
    count_il = lax.axis_size("il")
    count_xl = lax.axis_size("xl")
    devices = count_il * count_xl
    samples = traces.shape[1]
    row_block = slot_cells.shape[3]
    capacity = slot_block.shape[2]
    surveys = filter_taps.shape[0]
    blocks_here = traces.shape[0] // row_block
    cell_count = CIL * CXL
    group_size = 16
    slot_total = devices * capacity
    group_count = slot_total // group_size
    matrices = filter_matrices(filter_taps, samples)
    by_survey = traces.reshape(surveys, blocks_here // surveys * row_block, samples)
    filtered = jnp.einsum("sru,sut->srt", by_survey, matrices, preferred_element_type=jnp.float32)
    filtered = filtered.astype(jnp.bfloat16).reshape(blocks_here, row_block, samples)
    block_ids = slot_block[0].reshape(-1)
    outgoing = jnp.take(filtered, block_ids, axis=0).reshape(devices, capacity, row_block, samples)
    slot_live = jnp.arange(capacity, dtype=jnp.int32)[None, :] < pair_count[0][:, None]
    out_cells = jnp.where(slot_live[:, :, None], slot_cells[0], -1)
    incoming, in_cells = (
        lax.all_to_all(outgoing, ("il", "xl"), split_axis=0, concat_axis=0, tiled=True),
        lax.all_to_all(out_cells, ("il", "xl"), split_axis=0, concat_axis=0, tiled=True),
    )
    incoming = incoming.reshape(slot_total, row_block, samples)
    in_cells = in_cells.reshape(slot_total, row_block)
    cell_line = jnp.arange(cell_count, dtype=jnp.int32)

    def one_hot(group_cells):
        return (cell_line[:, None] == group_cells.reshape(1, -1)).astype(jnp.bfloat16)

    def add_group(running, group_blocks, group_cells):
        stacked, fold_counts = running
        selector = one_hot(group_cells)
        stacked = stacked + jnp.dot(
            selector, group_blocks.reshape(-1, samples), preferred_element_type=jnp.float32
        )
        fold_counts = fold_counts + jnp.sum(selector, axis=1, dtype=jnp.float32)
        return (stacked, fold_counts)

    initial = (jnp.zeros((cell_count, samples), jnp.float32), jnp.zeros((cell_count,), jnp.float32))

    def scan_step(running, scan_item):
        return (add_group(running, scan_item[0], scan_item[1]), None)

    (stacked, fold_counts), unused = lax.scan(
        scan_step,
        initial,
        (
            incoming.reshape(group_count, group_size, row_block, samples),
            in_cells.reshape(group_count, group_size, row_block),
        ),
    )
    stack_image = stacked / jnp.maximum(fold_counts, 1.0)[:, None]
    image_half = stack_image.astype(jnp.bfloat16)

    def read_group(group_cells):
        selector = one_hot(group_cells)
        picked = lax.dot_general(
            selector, image_half, (((0,), (0,)), ((), ())), preferred_element_type=jnp.float32
        )
        return picked.astype(jnp.bfloat16).reshape(group_size, row_block, samples)

    answer = lax.map(read_group, in_cells.reshape(group_count, group_size, row_block)).reshape(
        slot_total, row_block, samples
    )
    returned = lax.all_to_all(
        answer.reshape(devices, capacity, row_block, samples),
        ("il", "xl"),
        split_axis=0,
        concat_axis=0,
        tiled=True,
    )
    returned = returned.reshape(slot_total, row_block, samples)
    out_valid = (out_cells >= 0).reshape(slot_total, row_block, 1)
    zero_half = jnp.zeros((), jnp.bfloat16)
    sent_part = jnp.where(out_valid, outgoing.reshape(slot_total, row_block, samples), zero_half)
    back_part = jnp.where(out_valid, returned, zero_half)
    selector_rows = (
        block_ids[:, None] == jnp.arange(blocks_here, dtype=jnp.int32)[None, :]
    ).astype(jnp.bfloat16)
    residual = jnp.einsum(
        "sb,sit->bit", selector_rows, sent_part, preferred_element_type=jnp.float32
    )
    residual = residual - jnp.einsum(
        "sb,sit->bit", selector_rows, back_part, preferred_element_type=jnp.float32
    )
    residual_half = residual.astype(jnp.bfloat16).reshape(surveys, -1, samples)
    adjoint_traces = jnp.einsum(
        "srt,sut->sru", residual_half, matrices, preferred_element_type=jnp.float32
    ).reshape(traces.shape)
    padded = with_halo(
        stack_image.reshape(CIL, CXL, samples), (("il", count_il, 0), ("xl", count_xl, 1)), 2
    )
    structure_tensor = tensor(
        padded, (count_il, lax.axis_index("il")), (count_xl, lax.axis_index("xl"))
    )
    return (structure_tensor, adjoint_traces)


def solution(mesh):
    inner, names, body = mesh, (("il",), ("xl",)), local
    if mesh.devices.shape == (4, 8):
        inner = Mesh(mesh.devices.reshape(2, 2, 4, 2), ("x", "c", "z", "y"))
        names, body = (("x", "c"), ("z", "y")), local_planes
    il, xl = names
    both = il + xl
    return jax.shard_map(
        body,
        mesh=inner,
        in_specs=(
            P(both, None),
            P(),
            P(both, None, None),
            P(both, None, None, None),
            P(both, None),
        ),
        out_specs=(P(None, il, xl, None), P(both, None)),
        check_vma=False,
    )
```

```python
import functools

import jax
import jax.numpy as jnp
from jax import lax
from jax.experimental import pallas as pl
from jax.experimental.pallas import tpu as pltpu
from jax.sharding import Mesh
from jax.sharding import PartitionSpec as P

CIL = 32
CXL = 48
CELLS = CIL * CXL
QUARTER = CELLS // 4
FOLD = CXL // 3
MIB = 1 << 20
VMEM_LIMIT = 62 * MIB
IN_SMEM = pl.BlockSpec(memory_space=pltpu.SMEM)
IN_VMEM = pl.BlockSpec(memory_space=pltpu.VMEM)
IN_ANY = pl.BlockSpec(memory_space=pl.ANY)
IN_HBM = pl.BlockSpec(memory_space=pltpu.HBM)

WEIGHT = pl.CostEstimate(flops=1 << 35, bytes_accessed=1 << 20, transcendentals=0)
LIGHT = pl.CostEstimate(flops=1, bytes_accessed=1, transcendentals=0)


def hot(cells, shape, axis):
    line = lax.broadcasted_iota(jnp.int32, shape, axis)
    return jnp.where(line == cells, 1.0, 0.0).astype(jnp.bfloat16)


def quarter_of(cells):
    return sum((cells >= q * QUARTER).astype(jnp.int32) for q in (1, 2, 3))


def low_lanes(shape):
    return lax.broadcasted_iota(jnp.int32, shape, len(shape) - 1) < 64


def swap_lanes(value):
    return pltpu.roll(value, 64, 1)


def tie(values, *tokens):
    count = len(values)

    def kernel(*refs):
        pass

    return pl.pallas_call(
        kernel,
        out_shape=[jax.ShapeDtypeStruct(value.shape, value.dtype) for value in values],
        in_specs=[IN_ANY] * (count + len(tokens)),
        out_specs=[IN_ANY] * count,
        input_output_aliases={i: i for i in range(count)},
        cost_estimate=LIGHT,
        compiler_params=pltpu.CompilerParams(vmem_limit_bytes=VMEM_LIMIT),
        name="tie",
    )(*values, *tokens)


def gate_kernel(skip, from_x, from_y, *refs):
    turn_x, turn_y, held, sems = refs[skip + 2 :]
    middle = turn_x.shape[0]
    copies = [
        pltpu.make_async_copy(from_x.at[pl.ds(0, middle)], held.at[0], sems.at[0]),
        pltpu.make_async_copy(from_y.at[pl.ds(middle, middle)], held.at[1], sems.at[1]),
    ]
    sends = [
        pltpu.make_async_copy(held.at[0], turn_x, sems.at[2]),
        pltpu.make_async_copy(held.at[1], turn_y, sems.at[3]),
    ]
    for copy in copies:
        copy.start()
    for copy, send in zip(copies, sends, strict=True):
        copy.wait()
        send.start()
    for send in sends:
        send.wait()


def gate(from_x, from_y, *tokens):
    full = jax.ShapeDtypeStruct(from_x.shape, from_x.dtype)
    part = jax.ShapeDtypeStruct((from_x.shape[0] // 2, from_x.shape[1]), from_x.dtype)
    return pl.pallas_call(
        functools.partial(gate_kernel, len(tokens)),
        out_shape=[full, full, part, part],
        in_specs=[IN_HBM] * 2 + [IN_ANY] * len(tokens),
        out_specs=[IN_HBM] * 4,
        input_output_aliases={0: 0, 1: 1},
        scratch_shapes=[
            pltpu.VMEM((2,) + part.shape, part.dtype),
            pltpu.SemaphoreType.DMA((4,)),
        ],
        compiler_params=pltpu.CompilerParams(vmem_limit_bytes=VMEM_LIMIT),
        name="gate",
    )(from_x, from_y, *tokens)


def filter_kernel(half, skip, taps, source, *refs):
    out, *matrices = refs[skip:]
    each, rows, samples = source.shape
    row = lax.broadcasted_iota(jnp.int32, (samples, samples), 0)
    col = lax.broadcasted_iota(jnp.int32, (samples, samples), 1)
    rest = jnp.zeros((1, samples - taps.shape[1]), jnp.float32)
    for i in range(each):
        line = taps[pl.ds(pl.program_id(0) * each + i, 1), :]
        line = jnp.broadcast_to(jnp.concatenate([line, rest], axis=1), (samples, samples))
        band = pltpu.roll(line, 0, 1, stride=1, stride_axis=0)
        matrix = jnp.where(col >= row, band, 0.0)
        if matrices:
            matrices[0][i] = matrix.astype(jnp.bfloat16)
        turned = matrix.T[64 * half : 64 * half + 64].astype(jnp.bfloat16)
        value = lax.dot_general(
            turned, source[i], (((1,), (1,)), ((), ())), preferred_element_type=jnp.float32
        ).astype(jnp.bfloat16)
        for block in range(rows // 128):
            out[i, 64 * block : 64 * block + 64] = value[:, 128 * block : 128 * block + 128]


def filter_call(half, traces, taps, tokens=()):
    surveys = taps.shape[0]
    samples = traces.shape[1]
    rows = traces.shape[0] // surveys
    each = 3
    out_specs = [pl.BlockSpec((each, rows // 2, samples), lambda i: (i, 0, 0))]
    out_shape = [jax.ShapeDtypeStruct((surveys, rows // 2, samples), jnp.bfloat16)]
    if half == 1:
        out_specs.append(pl.BlockSpec((each, samples, samples), lambda i: (i, 0, 0)))
        out_shape.append(jax.ShapeDtypeStruct((surveys, samples, samples), jnp.bfloat16))
    return pl.pallas_call(
        functools.partial(filter_kernel, half, len(tokens)),
        grid=(surveys // each,),
        in_specs=[
            pl.BlockSpec(taps.shape, lambda i: (0, 0)),
            pl.BlockSpec((each, rows, samples), lambda i: (i, 0, 0)),
        ]
        + [IN_ANY] * len(tokens),
        out_specs=out_specs,
        out_shape=out_shape,
        compiler_params=pltpu.CompilerParams(vmem_limit_bytes=VMEM_LIMIT),
        name=f"filter_{half}",
    )(taps, traces.reshape(surveys, rows, samples), *tokens)


def stack_kernel(spec, order, cells, *refs):
    sizes, sources, tiles, with_fold, first, last, skip, base = spec
    per_slot = cells.shape[1]
    group = 16
    pieces = refs[: len(sizes)]
    refs = refs[len(sizes) :]
    if not first:
        before, refs = refs[0], refs[1:]
    refs = refs[skip:]
    outs = refs[: tiles if last else 1]
    held, total, live, numbers, sems = refs[len(outs) :]
    copies = []
    start = 0
    for i, rows in enumerate(sizes):
        copies.append(
            pltpu.make_async_copy(pieces[i], held.at[pl.ds(start, rows)], sems.at[i])
        )
        start += rows
    per_source = start // sources
    if not first:
        copies.append(pltpu.make_async_copy(before, total, sems.at[len(sizes)]))
    origins = cells.shape[0]
    for i in range(origins):
        copies.append(
            pltpu.make_async_copy(
                cells.at[i, pl.ds(per_slot - 8, 8)],
                numbers.at[pl.ds(8 * i, 8)],
                sems.at[len(sizes) + 1 + tiles + i],
            )
        )
    for copy in copies:
        copy.start()
    if first:
        total[...] = jnp.zeros_like(total)
    for copy in copies:
        copy.wait()

    def tile_step(tile, unused):
        def add_source(source, n):
            origin = order[base + source]
            wanted = order[tile]

            def add_slot(c, n):
                live[n] = wanted * 8 + c
                live[n + 128] = numbers[origin * 8 + wanted, c] * 64 + source * per_source
                live[n + 256] = origin
                return n + 1

            return lax.fori_loop(0, numbers[origin * 8 + wanted, 7], add_slot, n)

        n = lax.fori_loop(0, sources, add_source, 0)

        def one_group(g, unused):
            picked, data, selector = [], [], []
            for i in range(group):
                at = g * group + i
                place = jnp.minimum(at, n - 1)
                row = jnp.where(at < n, cells[live[256 + place], pl.ds(live[place], 1), :], -1)
                quarter = quarter_of(row)
                block = held[pl.ds(pl.multiple_of(live[128 + place], 64), 64), :]
                block = block.astype(jnp.float32)
                data.append(
                    jnp.concatenate(
                        [jnp.where(quarter == q, block, 0.0) for q in range(4)], axis=0
                    ).astype(jnp.bfloat16)
                )
                selector.append(hot(row - QUARTER * quarter, (QUARTER, 128), 0))
                picked.append(row)
            total[tile, :QUARTER] += lax.dot_general(
                jnp.concatenate(selector, axis=1),
                jnp.concatenate(data, axis=1),
                (((1,), (1,)), ((), ())),
                preferred_element_type=jnp.float32,
            )
            line = jnp.concatenate(picked, axis=1)
            width = line.shape[1]
            if with_fold:
                inline = ((line >> 4) * 171) >> 9
                cross = line - CXL * inline
                row = jnp.where(line >= 0, cross & 15, -1)
                lane = inline + 32 * (cross >> 4)
                total[tile, QUARTER:, :128] += lax.dot_general(
                    hot(row, (FOLD, width), 0),
                    hot(lane, (128, width), 0),
                    (((1,), (1,)), ((), ())),
                    preferred_element_type=jnp.float32,
                )
            return 0

        lax.fori_loop(0, (n + group - 1) // group, one_group, 0)
        return 0

    lax.fori_loop(0, tiles, tile_step, 0)
    targets = [total.at[tile] for tile in range(tiles)] if last else [total]
    sends = [
        pltpu.make_async_copy(target, out, sems.at[len(sizes) + 1 + i])
        for i, (target, out) in enumerate(zip(targets, outs, strict=True))
    ]
    for send in sends:
        send.start()
    for send in sends:
        send.wait()


def stack_call(order, base, cells, pieces, sources, before, tiles, with_fold, last, tokens=()):
    first = before is None
    sizes = tuple(piece.shape[0] for piece in pieces)
    rows = QUARTER + (FOLD if with_fold else 0)
    extra = [] if first else [before]
    every = jax.ShapeDtypeStruct((tiles, rows, 256), jnp.float32)
    single = [jax.ShapeDtypeStruct((rows, 256), jnp.float32)] * tiles
    origins = cells.shape[0]
    spec = (sizes, sources, tiles, with_fold, first, last, len(tokens), base)
    return pl.pallas_call(
        functools.partial(stack_kernel, spec),
        out_shape=single if last else [every],
        in_specs=[IN_SMEM, IN_VMEM]
        + [IN_HBM] * (len(pieces) + len(extra))
        + [IN_ANY] * len(tokens),
        out_specs=[IN_HBM] * (tiles if last else 1),
        scratch_shapes=[
            pltpu.VMEM((sum(sizes), 128), jnp.bfloat16),
            pltpu.VMEM(every.shape, jnp.float32),
            pltpu.SMEM((384,), jnp.int32),
            pltpu.SMEM((8 * origins, 128), jnp.int32),
            pltpu.SemaphoreType.DMA((len(pieces) + 1 + tiles + origins,)),
        ],
        compiler_params=pltpu.CompilerParams(vmem_limit_bytes=VMEM_LIMIT),
        cost_estimate=LIGHT if last else WEIGHT,
        name="stack",
    )(order, cells, *pieces, *extra, *tokens)


def image_kernel(half, skip, *refs):
    parts, refs = refs[:4], refs[4:]
    if half == 0:
        packed, value_out, fold_out, turned = refs[skip:]
        fold = sum(parts[i][QUARTER:] for i in range(4))
        fold_out[...] = fold
    else:
        fold_in, before, packed, image, turned = refs[:2] + refs[2 + skip :]
        fold = fold_in[...]
    fold = jnp.maximum(fold, 1.0)
    left = low_lanes((CXL, 128))
    for a in range(CIL // 4):
        here = slice(a * CXL, (a + 1) * CXL)
        columns = []
        for q in range(4):
            lane = q * (CIL // 4) + a
            columns.append(
                jnp.concatenate(
                    [fold[:, 32 * j + lane : 32 * j + lane + 1] for j in range(3)], axis=0
                )
            )
        for side in range(2):
            lanes = slice(128 * side, 128 * side + 128)
            total = (parts[0][here, lanes] + parts[1][here, lanes]) + (
                parts[2][here, lanes] + parts[3][here, lanes]
            )
            value = total / jnp.where(left, columns[2 * side], columns[2 * side + 1])
            turned[here, lanes] = value
            if half == 0:
                value_out[here, lanes] = value
            else:
                earlier = before[here, lanes]
                even, odd = 2 * side * QUARTER + a * CXL, (2 * side + 1) * QUARTER + a * CXL
                image[even : even + CXL] = jnp.where(left, earlier, swap_lanes(value))
                image[odd : odd + CXL] = jnp.where(left, swap_lanes(earlier), value)
    copy = turned[...].T.astype(jnp.bfloat16)
    for i in range(4):
        packed[256 * i : 256 * i + 256] = copy


def image_call(half, parts, extra, tokens):
    packed = jax.ShapeDtypeStruct((4 * 256, QUARTER), jnp.bfloat16)
    if half == 0:
        out_shape = [
            packed,
            jax.ShapeDtypeStruct((QUARTER, 256), jnp.float32),
            jax.ShapeDtypeStruct((FOLD, 256), jnp.float32),
        ]
    else:
        out_shape = [packed, jax.ShapeDtypeStruct((CELLS, 128), jnp.float32)]
    return pl.pallas_call(
        functools.partial(image_kernel, half, len(tokens)),
        out_shape=out_shape,
        in_specs=[IN_VMEM] * (4 + len(extra)) + [IN_ANY] * len(tokens),
        out_specs=[IN_VMEM] * len(out_shape),
        scratch_shapes=[pltpu.VMEM((QUARTER, 256), jnp.float32)],
        cost_estimate=LIGHT,
        compiler_params=pltpu.CompilerParams(vmem_limit_bytes=VMEM_LIMIT),
        name=f"image_{half}",
    )(*parts, *extra, *tokens)


def read_kernel(spec, order, counts, blocks, cells, own, *refs):
    sizes, first, last, skip, base = spec
    group = 4
    tiles = sum(sizes) // 256
    pieces = refs[: len(sizes)]
    refs = refs[len(sizes) :]
    if last:
        matrices, earlier, refs = refs[0], refs[1], refs[2:]
    if not first:
        before, refs = refs[0], refs[1:]
    refs = refs[skip:]
    out, held, mine, total, live, sems = refs[:6]
    copies = [pltpu.make_async_copy(own, mine, sems.at[0])]
    if not first:
        copies.append(pltpu.make_async_copy(before, total, sems.at[len(sizes) + 1]))
    if last:
        whole_out, earlier_in, band = refs[6:]
        later = [
            pltpu.make_async_copy(earlier, earlier_in, sems.at[len(sizes) + 2]),
            pltpu.make_async_copy(matrices, band, sems.at[len(sizes) + 3]),
        ]
    start = 0
    for i, rows in enumerate(sizes):
        copies.append(
            pltpu.make_async_copy(pieces[i], held.at[pl.ds(start, rows)], sems.at[i + 1])
        )
        start += rows
    for copy in copies:
        copy.start()
    if first:
        total[...] = jnp.zeros_like(total)

    def add_tile(j, n):
        for g in range(8 // group):
            live[n] = order[base + j] * 8 + g * group
            live[n + 128] = j
            n = n + (counts[order[base + j]] > g * group).astype(jnp.int32)
        return n

    if last:
        for copy in later:
            copy.start()
    n = lax.fori_loop(0, tiles, add_tile, 0)
    for copy in copies:
        copy.wait()

    def one_step(step, unused):
        waiting = []
        for k in range(2):
            at = step * 2 + k
            place = jnp.minimum(at, n - 1)
            entry = live[place]
            rows = [
                jnp.where(at < n, cells[pl.ds(entry + i, 1), :], -1) for i in range(group)
            ]
            quarters = [quarter_of(row) for row in rows]
            selector = jnp.concatenate(
                [
                    hot(row - QUARTER * quarter, (QUARTER, 128), 0)
                    for row, quarter in zip(rows, quarters, strict=True)
                ],
                axis=1,
            )
            image = held[pl.ds(pl.multiple_of(live[128 + place] * 256, 256), 256), :]
            got = jnp.dot(image, selector, preferred_element_type=jnp.float32)
            waiting.append((entry, rows, quarters, got))
        for entry, rows, quarters, got in waiting:
            for i in range(group):
                here = pl.ds(pl.multiple_of(blocks[entry + i] * 64, 64), 64)
                part = got[:, 128 * i : 128 * i + 128]
                value = part[:64]
                for q in (1, 2, 3):
                    value = jnp.where(quarters[i] == q, part[64 * q : 64 * q + 64], value)
                sent = jnp.where(rows[i] >= 0, mine[here, :].astype(jnp.float32), 0.0)
                total[here, :] += sent - value
        return 0

    lax.fori_loop(0, (n + 1) // 2, one_step, 0)
    if not last:
        send = pltpu.make_async_copy(total, out, sems.at[len(sizes) + 4])
        send.start()
        send.wait()
        return
    for copy in later:
        copy.wait()
    surveys = matrices.shape[0]
    rows = whole_out.shape[0] // surveys
    sends = []
    for survey in range(surveys):
        for block in range(rows // 128):
            at = survey * (rows // 2) + block * 64
            residual = jnp.concatenate(
                [earlier_in[at : at + 64], total[at : at + 64]], axis=0
            ).T.astype(jnp.bfloat16)
            whole_out[survey * rows + 128 * block : survey * rows + 128 * block + 128] = (
                lax.dot_general(
                    residual,
                    band[survey],
                    (((1,), (1,)), ((), ())),
                    preferred_element_type=jnp.float32,
                )
            )
        sends.append(
            pltpu.make_async_copy(
                whole_out.at[pl.ds(survey * rows, rows)],
                out.at[pl.ds(survey * rows, rows)],
                sems.at[len(sizes) + 4 + survey],
            )
        )
        sends[-1].start()
    for send in sends:
        send.wait()


def read_call(
    order, base, slots, own, pieces, before, matrices=None, earlier=None, tokens=(), cost=None
):
    first, last = before is None, matrices is not None
    sizes = tuple(piece.shape[0] for piece in pieces)
    extra = ([matrices, earlier] if last else []) + ([] if first else [before])
    surveys = matrices.shape[0] if last else 0
    full = (2 * own.shape[0], own.shape[1])
    return pl.pallas_call(
        functools.partial(read_kernel, (sizes, first, last, len(tokens), base)),
        out_shape=jax.ShapeDtypeStruct(full if last else own.shape, jnp.float32),
        in_specs=[IN_SMEM] * 3
        + [IN_VMEM]
        + [IN_HBM] * (1 + len(pieces))
        + [IN_HBM] * len(extra)
        + [IN_ANY] * len(tokens),
        out_specs=IN_HBM,
        scratch_shapes=[
            pltpu.VMEM((sum(sizes), QUARTER), jnp.bfloat16),
            pltpu.VMEM(own.shape, jnp.bfloat16),
            pltpu.VMEM(own.shape, jnp.float32),
            pltpu.SMEM((256,), jnp.int32),
            pltpu.SemaphoreType.DMA((len(sizes) + 5 + surveys,)),
        ]
        + (
            [
                pltpu.VMEM(full, jnp.float32),
                pltpu.VMEM(own.shape, jnp.float32),
                pltpu.VMEM(matrices.shape, jnp.bfloat16),
            ]
            if last
            else []
        ),
        compiler_params=pltpu.CompilerParams(vmem_limit_bytes=VMEM_LIMIT),
        cost_estimate=cost or LIGHT,
        name="read",
    )(order, *slots, own, *pieces, *extra, *tokens)


def with_halo(block, sides, width):
    for axis, count, dim in sides:
        forward = [(i, i + 1) for i in range(count - 1)]
        backward = [(target, source) for source, target in forward]
        low = lax.ppermute(
            lax.slice_in_dim(block, block.shape[dim] - width, None, axis=dim), axis, forward
        )
        high = lax.ppermute(lax.slice_in_dim(block, 0, width, axis=dim), axis, backward)
        block = jnp.concatenate([low, block, high], axis=dim)
    return block


def cycle_box(values, rows_out, cols_out):
    box_total = jnp.zeros((rows_out, cols_out, values.shape[2]), jnp.float32)
    for row_shift in range(3):
        for col_shift in range(3):
            box_total = (
                box_total
                + values[row_shift : row_shift + rows_out, col_shift : col_shift + cols_out]
            )
    return box_total / 9.0


def tensor(padded, il, xl):
    count_il, at_il = il
    count_xl, at_xl = xl
    padded_time = jnp.pad(padded, ((0, 0), (0, 0), (1, 1)))
    grad_il = (padded[2:, 1:-1] - padded[:-2, 1:-1]) * 0.5
    grad_xl = (padded[1:-1, 2:] - padded[1:-1, :-2]) * 0.5
    grad_time = (padded_time[1:-1, 1:-1, 2:] - padded_time[1:-1, 1:-1, :-2]) * 0.5
    rows_il = at_il * CIL + jnp.arange(CIL + 2, dtype=jnp.int32) - 1
    rows_xl = at_xl * CXL + jnp.arange(CXL + 2, dtype=jnp.int32) - 1
    inside_il = ((rows_il >= 0) & (rows_il < CIL * count_il)).astype(jnp.float32)
    inside_xl = ((rows_xl >= 0) & (rows_xl < CXL * count_xl)).astype(jnp.float32)
    cycle_mask = inside_il[:, None, None] * inside_xl[None, :, None]
    factor_pairs = (
        (grad_il, grad_il),
        (grad_xl, grad_xl),
        (grad_time, grad_time),
        (grad_il, grad_xl),
        (grad_il, grad_time),
        (grad_xl, grad_time),
    )
    return jnp.stack(
        [
            cycle_box(left_part * right_part * cycle_mask, CIL, CXL)
            for left_part, right_part in factor_pairs
        ]
    )


def tensor_kernel(place, image, low_il, high_il, low_xl, high_xl, out, padded, boxed):
    padded[:2, 2 : CXL + 2] = low_il[...]
    padded[2 : CIL + 2, 2 : CXL + 2] = image[...]
    padded[CIL + 2 :, 2 : CXL + 2] = high_il[...]
    padded[:, :2] = low_xl[...]
    padded[:, CXL + 2 : CXL + 4] = high_xl[...]
    shape = (CXL + 2, 128)
    col = lax.broadcasted_iota(jnp.int32, shape, 0) + (place[2] * CXL - 1)
    lane = lax.broadcasted_iota(jnp.int32, shape, 1)
    inside = (col >= 0) & (col < CXL * place[3])

    def one_row(r, unused):
        row = place[0] * CIL + r - 1
        here = inside & (row >= 0) & (row < CIL * place[1])
        middle = padded[r + 1, 1 : CXL + 3]
        later = jnp.where(lane < 127, pltpu.roll(middle, 127, 1), 0.0)
        earlier = jnp.where(lane > 0, pltpu.roll(middle, 1, 1), 0.0)
        along = [
            (padded[r + 2, 1 : CXL + 3] - padded[r, 1 : CXL + 3]) * 0.5,
            (padded[r + 1, 2 : CXL + 4] - padded[r + 1, 0 : CXL + 2]) * 0.5,
            (later - earlier) * 0.5,
        ]
        along = [jnp.where(here, part, 0.0) for part in along]
        for k, (i, j) in enumerate(((0, 0), (1, 1), (2, 2), (0, 1), (0, 2), (1, 2))):
            product = along[i] * along[j]
            boxed[k, r] = (product[:CXL] + product[1 : CXL + 1]) + product[2:]
        return 0

    lax.fori_loop(0, CIL + 2, one_row, 0)

    def one_out(r, unused):
        for k in range(6):
            out[k, r] = ((boxed[k, r] + boxed[k, r + 1]) + boxed[k, r + 2]) / 9.0
        return 0

    lax.fori_loop(0, CIL, one_out, 0)


def tensor_call(place, image, halo, tokens=()):
    def kernel(*refs):
        tensor_kernel(*refs[:6], *refs[6 + len(tokens) :])

    return pl.pallas_call(
        kernel,
        out_shape=jax.ShapeDtypeStruct((6, CIL, CXL, 128), jnp.float32),
        in_specs=[IN_SMEM] + [IN_VMEM] * 5 + [IN_ANY] * len(tokens),
        out_specs=IN_VMEM,
        scratch_shapes=[
            pltpu.VMEM((CIL + 4, CXL + 8, 128), jnp.float32),
            pltpu.VMEM((6, CIL + 2, CXL, 128), jnp.float32),
        ],
        compiler_params=pltpu.CompilerParams(vmem_limit_bytes=VMEM_LIMIT),
        cost_estimate=LIGHT,
        name="tensor",
    )(place, image, *halo, *tokens)


def halo_of(image, side_il, side_xl):
    axis_il, count_il = side_il
    axis_xl, count_xl = side_xl
    up_il, up_xl = ([(i, i + 1) for i in range(n - 1)] for n in (count_il, count_xl))
    down_il, down_xl = ([(j, i) for i, j in up] for up in (up_il, up_xl))
    low_il = lax.ppermute(image[-2:], axis_il, up_il)
    high_il = lax.ppermute(image[:2], axis_il, down_il)

    def edge(cols):
        return jnp.concatenate([part[:, cols] for part in (low_il, image, high_il)], axis=0)

    low_xl = lax.ppermute(edge(slice(CXL - 2, CXL)), axis_xl, up_xl)
    high_xl = lax.ppermute(edge(slice(0, 2)), axis_xl, down_xl)
    return low_il, high_il, low_xl, high_xl


SWAP = [(0, 1), (1, 0)]


def along_z(value, step):
    return lax.ppermute(value, "z", [(i, (i + step) % 4) for i in range(4)])


def over(axis, value):
    return lax.ppermute(value, axis, SWAP)


def local_planes(traces, filter_taps, slot_block, slot_cells, pair_count):
    row_block = slot_cells.shape[3]
    capacity = slot_block.shape[2]
    samples = traces.shape[1]
    surveys, tap_count = filter_taps.shape
    x, core, z, y = (lax.axis_index(name) for name in ("x", "c", "z", "y"))
    other = 1 - core

    slot_live = jnp.arange(capacity, dtype=jnp.int32)[None, :] < pair_count[0][:, None]
    out_cells = jnp.where(slot_live[:, :, None], slot_cells[0], -1)
    own_cells = jnp.pad(out_cells, ((0, 0), (0, 1), (0, 0)), constant_values=-1)
    numbers = jnp.concatenate([slot_block[0], pair_count[0][:, None]], axis=1)

    def by_column(value):
        parts = value.reshape((2, 2, 4, 2) + value.shape[1:])
        return jnp.moveaxis(parts, 2, 3).reshape((8, 4) + value.shape[1:])

    arrived = lax.all_to_all(
        jnp.concatenate(
            [
                by_column(own_cells).reshape(8, 32, row_block),
                jnp.pad(by_column(numbers), ((0, 0), (0, 4), (0, row_block - 8))),
            ],
            axis=1,
        ),
        ("x", "c", "y"),
        0,
        0,
        tiled=True,
    )
    own_slots = (pair_count[0], numbers.reshape(256), own_cells.reshape(256, row_block))

    rows_half = traces.shape[0] // 2
    (first_half,) = filter_call(0, traces, filter_taps)
    second_half, matrices = filter_call(1, traces, filter_taps)
    halves = [part.reshape(rows_half, samples) for part in (first_half, second_half)]

    spots = ((x, y), (1 - x, y), (x, 1 - y), (1 - x, 1 - y))
    orders = [lax.rem(z + step, 4) for step in range(4)]
    for at_x, at_y in spots:
        orders += [(at_x * 2 + at_core) * 2 + at_y for at_core in (core, other)]
    wanted = [(spot, core) for spot in spots[:3]] + [(spot, other) for spot in spots[:3]]
    wanted += [(spots[3], core), (spots[3], other)]
    wanted += [(spot, at_core) for spot in spots[:3] for at_core in (core, other)]
    for (at_x, at_y), at_core in wanted:
        orders += [((at_x * 2 + at_core) * 4 + at_z) * 2 + at_y for at_z in range(4)]
    orders = jnp.stack(orders)

    def spread(value, *tokens):
        from_x, from_y, turn_x, turn_y = gate(over("x", value), over("y", value), *tokens)
        return from_x, from_y, (over("y", turn_x), over("x", turn_y))

    def pairs(*pieces):
        return [part for piece in pieces for part in (piece, over("c", piece))]

    def near_stack(half, pieces, tokens=()):
        return stack_call(orders, 4, arrived, pieces, 6, None, 4, half == 0, False, tokens)[0]

    def far_stack(half, parts, before):
        pieces = [*parts, *(over("c", part) for part in parts)]
        return stack_call(orders, 10, arrived, pieces, 2, before, 4, half == 0, True)

    def sum_z(partial):
        return [partial[0]] + [along_z(partial[step], step) for step in (2, 1, 3)]

    def over_z(value):
        return lax.all_to_all(value, "z", 0, 0, tiled=True)

    def read(half, base, pieces, *rest, **named):
        return read_call(orders, base, own_slots, halves[half], pieces, *rest, **named)


    from_x, from_y, parts = spread(halves[0], halves[1], arrived, orders, *own_slots)
    near_0 = near_stack(0, pairs(halves[0], from_x, from_y))
    (own_1,) = tie([halves[1]], near_0)
    halves[1] = own_1
    partial_0 = far_stack(0, tie(parts, near_0), near_0)
    packed_0, stacked, fold = image_call(0, sum_z(partial_0), [], [])
    from_x, from_y, parts = spread(own_1, packed_0)
    columns_0 = over_z(tie([packed_0], from_x)[0])
    near_1 = near_stack(1, pairs(own_1, from_x, from_y))
    partial_1 = far_stack(1, tie(parts, near_1), near_1)
    (columns_0,) = tie([columns_0], partial_1[0])
    from_x, from_y, parts = spread(columns_0)
    own_layers = [columns_0, from_x, from_y]
    residual_0 = read(0, 12, own_layers, None)
    packed_1, image = image_call(1, sum_z(partial_1), [fold, stacked], [residual_0, *parts])
    columns_1 = over_z(packed_1)
    image = image.reshape(CIL, CXL, samples)
    halo = halo_of(image, (("x", "c"), 4), (("z", "y"), 8))
    place = jnp.stack([x * 2 + core, jnp.int32(4), z * 2 + y, jnp.int32(8)])
    own_layers = tie([*own_layers, *parts], packed_1)
    layers = [over("c", layer) for layer in own_layers]
    layers = layers[:3] + list(own_layers[3:]) + layers[3:]
    residual_0 = read(0, 24, layers, residual_0, tokens=[columns_1, *halo])
    structure_tensor = tensor_call(place, image, halo, [residual_0])
    from_x, from_y, parts = spread(columns_1, structure_tensor)
    residual_1 = read(1, 44, pairs(columns_1, from_x, from_y), None)
    parts = tie(parts, residual_1)
    layers = [*parts, *(over("c", part) for part in parts)]
    adjoint_traces = read(1, 36, layers, residual_1, matrices, residual_0)
    return (structure_tensor, adjoint_traces)


def filter_matrices(filter_taps, samples):
    lag_table = (
        jnp.arange(samples, dtype=jnp.int32)[None, :]
        - jnp.arange(samples, dtype=jnp.int32)[:, None]
    )
    tap_count = filter_taps.shape[1]
    inside = (lag_table >= 0) & (lag_table < tap_count)
    picked = filter_taps[:, jnp.clip(lag_table, 0, tap_count - 1)]
    return jnp.where(inside[None], picked, 0.0).astype(jnp.bfloat16)


def local(traces, filter_taps, slot_block, slot_cells, pair_count):
    count_il = lax.axis_size("il")
    count_xl = lax.axis_size("xl")
    devices = count_il * count_xl
    samples = traces.shape[1]
    row_block = slot_cells.shape[3]
    capacity = slot_block.shape[2]
    surveys = filter_taps.shape[0]
    blocks_here = traces.shape[0] // row_block
    cell_count = CIL * CXL
    group_size = 16
    slot_total = devices * capacity
    group_count = slot_total // group_size
    matrices = filter_matrices(filter_taps, samples)
    by_survey = traces.reshape(surveys, blocks_here // surveys * row_block, samples)
    filtered = jnp.einsum("sru,sut->srt", by_survey, matrices, preferred_element_type=jnp.float32)
    filtered = filtered.astype(jnp.bfloat16).reshape(blocks_here, row_block, samples)
    block_ids = slot_block[0].reshape(-1)
    outgoing = jnp.take(filtered, block_ids, axis=0).reshape(devices, capacity, row_block, samples)
    slot_live = jnp.arange(capacity, dtype=jnp.int32)[None, :] < pair_count[0][:, None]
    out_cells = jnp.where(slot_live[:, :, None], slot_cells[0], -1)
    incoming, in_cells = (
        lax.all_to_all(outgoing, ("il", "xl"), split_axis=0, concat_axis=0, tiled=True),
        lax.all_to_all(out_cells, ("il", "xl"), split_axis=0, concat_axis=0, tiled=True),
    )
    incoming = incoming.reshape(slot_total, row_block, samples)
    in_cells = in_cells.reshape(slot_total, row_block)
    cell_line = jnp.arange(cell_count, dtype=jnp.int32)

    def one_hot(group_cells):
        return (cell_line[:, None] == group_cells.reshape(1, -1)).astype(jnp.bfloat16)

    def add_group(running, group_blocks, group_cells):
        stacked, fold_counts = running
        selector = one_hot(group_cells)
        stacked = stacked + jnp.dot(
            selector, group_blocks.reshape(-1, samples), preferred_element_type=jnp.float32
        )
        fold_counts = fold_counts + jnp.sum(selector, axis=1, dtype=jnp.float32)
        return (stacked, fold_counts)

    initial = (jnp.zeros((cell_count, samples), jnp.float32), jnp.zeros((cell_count,), jnp.float32))

    def scan_step(running, scan_item):
        return (add_group(running, scan_item[0], scan_item[1]), None)

    (stacked, fold_counts), unused = lax.scan(
        scan_step,
        initial,
        (
            incoming.reshape(group_count, group_size, row_block, samples),
            in_cells.reshape(group_count, group_size, row_block),
        ),
    )
    stack_image = stacked / jnp.maximum(fold_counts, 1.0)[:, None]
    image_half = stack_image.astype(jnp.bfloat16)

    def read_group(group_cells):
        selector = one_hot(group_cells)
        picked = lax.dot_general(
            selector, image_half, (((0,), (0,)), ((), ())), preferred_element_type=jnp.float32
        )
        return picked.astype(jnp.bfloat16).reshape(group_size, row_block, samples)

    answer = lax.map(read_group, in_cells.reshape(group_count, group_size, row_block)).reshape(
        slot_total, row_block, samples
    )
    returned = lax.all_to_all(
        answer.reshape(devices, capacity, row_block, samples),
        ("il", "xl"),
        split_axis=0,
        concat_axis=0,
        tiled=True,
    )
    returned = returned.reshape(slot_total, row_block, samples)
    out_valid = (out_cells >= 0).reshape(slot_total, row_block, 1)
    zero_half = jnp.zeros((), jnp.bfloat16)
    sent_part = jnp.where(out_valid, outgoing.reshape(slot_total, row_block, samples), zero_half)
    back_part = jnp.where(out_valid, returned, zero_half)
    selector_rows = (
        block_ids[:, None] == jnp.arange(blocks_here, dtype=jnp.int32)[None, :]
    ).astype(jnp.bfloat16)
    residual = jnp.einsum(
        "sb,sit->bit", selector_rows, sent_part, preferred_element_type=jnp.float32
    )
    residual = residual - jnp.einsum(
        "sb,sit->bit", selector_rows, back_part, preferred_element_type=jnp.float32
    )
    residual_half = residual.astype(jnp.bfloat16).reshape(surveys, -1, samples)
    adjoint_traces = jnp.einsum(
        "srt,sut->sru", residual_half, matrices, preferred_element_type=jnp.float32
    ).reshape(traces.shape)
    padded = with_halo(
        stack_image.reshape(CIL, CXL, samples), (("il", count_il, 0), ("xl", count_xl, 1)), 2
    )
    structure_tensor = tensor(
        padded, (count_il, lax.axis_index("il")), (count_xl, lax.axis_index("xl"))
    )
    return (structure_tensor, adjoint_traces)


def solution(mesh):
    inner, names, body = mesh, (("il",), ("xl",)), local
    if mesh.devices.shape == (4, 8):
        inner = Mesh(mesh.devices.reshape(2, 2, 4, 2), ("x", "c", "z", "y"))
        names, body = (("x", "c"), ("z", "y")), local_planes
    il, xl = names
    both = il + xl
    return jax.shard_map(
        body,
        mesh=inner,
        in_specs=(
            P(both, None),
            P(),
            P(both, None, None),
            P(both, None, None, None),
            P(both, None),
        ),
        out_specs=(P(None, il, xl, None), P(both, None)),
        check_vma=False,
    )
```

```python
import functools

import jax
import jax.numpy as jnp
from jax import lax
from jax.experimental import pallas as pl
from jax.experimental.pallas import tpu as pltpu
from jax.sharding import Mesh
from jax.sharding import PartitionSpec as P

CIL = 32
CXL = 48
CELLS = CIL * CXL
QUARTER = CELLS // 4
FOLD = CXL // 3
MIB = 1 << 20
VMEM_LIMIT = 62 * MIB
IN_SMEM = pl.BlockSpec(memory_space=pltpu.SMEM)
IN_VMEM = pl.BlockSpec(memory_space=pltpu.VMEM)
IN_ANY = pl.BlockSpec(memory_space=pl.ANY)
IN_HBM = pl.BlockSpec(memory_space=pltpu.HBM)

WEIGHT = pl.CostEstimate(flops=1 << 35, bytes_accessed=1 << 20, transcendentals=0)
LIGHT = pl.CostEstimate(flops=1, bytes_accessed=1, transcendentals=0)


def hot(cells, shape, axis):
    line = lax.broadcasted_iota(jnp.int32, shape, axis)
    return jnp.where(line == cells, 1.0, 0.0).astype(jnp.bfloat16)


def quarter_of(cells):
    return sum((cells >= q * QUARTER).astype(jnp.int32) for q in (1, 2, 3))


def low_lanes(shape):
    return lax.broadcasted_iota(jnp.int32, shape, len(shape) - 1) < 64


def swap_lanes(value):
    return pltpu.roll(value, 64, 1)


def tie(values, *tokens):
    count = len(values)

    def kernel(*refs):
        pass

    return pl.pallas_call(
        kernel,
        out_shape=[jax.ShapeDtypeStruct(value.shape, value.dtype) for value in values],
        in_specs=[IN_ANY] * (count + len(tokens)),
        out_specs=[IN_ANY] * count,
        input_output_aliases={i: i for i in range(count)},
        cost_estimate=LIGHT,
        compiler_params=pltpu.CompilerParams(vmem_limit_bytes=VMEM_LIMIT),
        name="tie",
    )(*values, *tokens)


def gate_kernel(skip, from_x, from_y, *refs):
    turn_x, turn_y, held, sems = refs[skip + 2 :]
    middle = turn_x.shape[0]
    copies = [
        pltpu.make_async_copy(from_x.at[pl.ds(0, middle)], held.at[0], sems.at[0]),
        pltpu.make_async_copy(from_y.at[pl.ds(middle, middle)], held.at[1], sems.at[1]),
    ]
    sends = [
        pltpu.make_async_copy(held.at[0], turn_x, sems.at[2]),
        pltpu.make_async_copy(held.at[1], turn_y, sems.at[3]),
    ]
    for copy in copies:
        copy.start()
    for copy, send in zip(copies, sends, strict=True):
        copy.wait()
        send.start()
    for send in sends:
        send.wait()


def gate(from_x, from_y, *tokens):
    full = jax.ShapeDtypeStruct(from_x.shape, from_x.dtype)
    part = jax.ShapeDtypeStruct((from_x.shape[0] // 2, from_x.shape[1]), from_x.dtype)
    return pl.pallas_call(
        functools.partial(gate_kernel, len(tokens)),
        out_shape=[full, full, part, part],
        in_specs=[IN_HBM] * 2 + [IN_ANY] * len(tokens),
        out_specs=[IN_HBM] * 4,
        input_output_aliases={0: 0, 1: 1},
        scratch_shapes=[
            pltpu.VMEM((2,) + part.shape, part.dtype),
            pltpu.SemaphoreType.DMA((4,)),
        ],
        compiler_params=pltpu.CompilerParams(vmem_limit_bytes=VMEM_LIMIT),
        name="gate",
    )(from_x, from_y, *tokens)


def filter_kernel(half, skip, taps, source, *refs):
    out, *matrices = refs[skip:]
    each, rows, samples = source.shape
    row = lax.broadcasted_iota(jnp.int32, (samples, samples), 0)
    col = lax.broadcasted_iota(jnp.int32, (samples, samples), 1)
    rest = jnp.zeros((1, samples - taps.shape[1]), jnp.float32)
    for i in range(each):
        line = taps[pl.ds(pl.program_id(0) * each + i, 1), :]
        line = jnp.broadcast_to(jnp.concatenate([line, rest], axis=1), (samples, samples))
        band = pltpu.roll(line, 0, 1, stride=1, stride_axis=0)
        matrix = jnp.where(col >= row, band, 0.0)
        if matrices:
            matrices[0][i] = matrix.astype(jnp.bfloat16)
        turned = matrix.T[64 * half : 64 * half + 64].astype(jnp.bfloat16)
        value = lax.dot_general(
            turned, source[i], (((1,), (1,)), ((), ())), preferred_element_type=jnp.float32
        ).astype(jnp.bfloat16)
        for block in range(rows // 128):
            out[i, 64 * block : 64 * block + 64] = value[:, 128 * block : 128 * block + 128]


def filter_call(half, traces, taps, tokens=()):
    surveys = taps.shape[0]
    samples = traces.shape[1]
    rows = traces.shape[0] // surveys
    each = 6
    out_specs = [pl.BlockSpec((each, rows // 2, samples), lambda i: (i, 0, 0))]
    out_shape = [jax.ShapeDtypeStruct((surveys, rows // 2, samples), jnp.bfloat16)]
    if half == 1:
        out_specs.append(pl.BlockSpec((each, samples, samples), lambda i: (i, 0, 0)))
        out_shape.append(jax.ShapeDtypeStruct((surveys, samples, samples), jnp.bfloat16))
    return pl.pallas_call(
        functools.partial(filter_kernel, half, len(tokens)),
        grid=(surveys // each,),
        in_specs=[
            pl.BlockSpec(taps.shape, lambda i: (0, 0)),
            pl.BlockSpec((each, rows, samples), lambda i: (i, 0, 0)),
        ]
        + [IN_ANY] * len(tokens),
        out_specs=out_specs,
        out_shape=out_shape,
        compiler_params=pltpu.CompilerParams(vmem_limit_bytes=VMEM_LIMIT),
        name=f"filter_{half}",
    )(taps, traces.reshape(surveys, rows, samples), *tokens)


def stack_kernel(spec, order, cells, *refs):
    sizes, sources, tiles, with_fold, first, last, skip, base = spec
    per_slot = cells.shape[1]
    group = 16
    pieces = refs[: len(sizes)]
    refs = refs[len(sizes) :]
    if not first:
        before, refs = refs[0], refs[1:]
    refs = refs[skip:]
    outs = refs[: tiles if last else 1]
    held, total, live, numbers, sems = refs[len(outs) :]
    copies = []
    start = 0
    for i, rows in enumerate(sizes):
        copies.append(
            pltpu.make_async_copy(pieces[i], held.at[pl.ds(start, rows)], sems.at[i])
        )
        start += rows
    per_source = start // sources
    if not first:
        copies.append(pltpu.make_async_copy(before, total, sems.at[len(sizes)]))
    origins = cells.shape[0]
    for i in range(origins):
        copies.append(
            pltpu.make_async_copy(
                cells.at[i, pl.ds(per_slot - 8, 8)],
                numbers.at[pl.ds(8 * i, 8)],
                sems.at[len(sizes) + 1 + tiles + i],
            )
        )
    for copy in copies:
        copy.start()
    if first:
        total[...] = jnp.zeros_like(total)
    for copy in copies:
        copy.wait()

    def tile_step(tile, unused):
        def add_source(source, n):
            origin = order[base + source]
            wanted = order[tile]

            def add_slot(c, n):
                live[n] = wanted * 8 + c
                live[n + 128] = numbers[origin * 8 + wanted, c] * 64 + source * per_source
                live[n + 256] = origin
                return n + 1

            return lax.fori_loop(0, numbers[origin * 8 + wanted, 7], add_slot, n)

        n = lax.fori_loop(0, sources, add_source, 0)

        def one_group(g, unused):
            picked, data, selector = [], [], []
            for i in range(group):
                at = g * group + i
                place = jnp.minimum(at, n - 1)
                row = jnp.where(at < n, cells[live[256 + place], pl.ds(live[place], 1), :], -1)
                quarter = quarter_of(row)
                block = held[pl.ds(pl.multiple_of(live[128 + place], 64), 64), :]
                block = block.astype(jnp.float32)
                data.append(
                    jnp.concatenate(
                        [jnp.where(quarter == q, block, 0.0) for q in range(4)], axis=0
                    ).astype(jnp.bfloat16)
                )
                selector.append(hot(row - QUARTER * quarter, (QUARTER, 128), 0))
                picked.append(row)
            total[tile, :QUARTER] += lax.dot_general(
                jnp.concatenate(selector, axis=1),
                jnp.concatenate(data, axis=1),
                (((1,), (1,)), ((), ())),
                preferred_element_type=jnp.float32,
            )
            line = jnp.concatenate(picked, axis=1)
            width = line.shape[1]
            if with_fold:
                inline = ((line >> 4) * 171) >> 9
                cross = line - CXL * inline
                row = jnp.where(line >= 0, cross & 15, -1)
                lane = inline + 32 * (cross >> 4)
                total[tile, QUARTER:, :128] += lax.dot_general(
                    hot(row, (FOLD, width), 0),
                    hot(lane, (128, width), 0),
                    (((1,), (1,)), ((), ())),
                    preferred_element_type=jnp.float32,
                )
            return 0

        lax.fori_loop(0, (n + group - 1) // group, one_group, 0)
        return 0

    targets = [total.at[tile] for tile in range(tiles)] if last else [total]
    sends = [
        pltpu.make_async_copy(target, out, sems.at[len(sizes) + 1 + i])
        for i, (target, out) in enumerate(zip(targets, outs, strict=True))
    ]
    if last:
        for tile, send in enumerate(sends):
            tile_step(tile, 0)
            send.start()
    else:
        lax.fori_loop(0, tiles, tile_step, 0)
        sends[0].start()
    for send in sends:
        send.wait()


def stack_call(order, base, cells, pieces, sources, before, tiles, with_fold, last, tokens=()):
    first = before is None
    sizes = tuple(piece.shape[0] for piece in pieces)
    rows = QUARTER + (FOLD if with_fold else 0)
    extra = [] if first else [before]
    every = jax.ShapeDtypeStruct((tiles, rows, 256), jnp.float32)
    single = [jax.ShapeDtypeStruct((rows, 256), jnp.float32)] * tiles
    origins = cells.shape[0]
    spec = (sizes, sources, tiles, with_fold, first, last, len(tokens), base)
    return pl.pallas_call(
        functools.partial(stack_kernel, spec),
        out_shape=single if last else [every],
        in_specs=[IN_SMEM, IN_VMEM]
        + [IN_HBM] * (len(pieces) + len(extra))
        + [IN_ANY] * len(tokens),
        out_specs=[IN_HBM] * (tiles if last else 1),
        scratch_shapes=[
            pltpu.VMEM((sum(sizes), 128), jnp.bfloat16),
            pltpu.VMEM(every.shape, jnp.float32),
            pltpu.SMEM((384,), jnp.int32),
            pltpu.SMEM((8 * origins, 128), jnp.int32),
            pltpu.SemaphoreType.DMA((len(pieces) + 1 + tiles + origins,)),
        ],
        compiler_params=pltpu.CompilerParams(vmem_limit_bytes=VMEM_LIMIT),
        cost_estimate=LIGHT if last else WEIGHT,
        name="stack",
    )(order, cells, *pieces, *extra, *tokens)


def image_kernel(half, skip, *refs):
    parts, refs = refs[:4], refs[4:]
    if half == 0:
        packed, value_out, fold_out, turned = refs[skip:]
        fold = sum(parts[i][QUARTER:] for i in range(4))
        fold_out[...] = fold
    else:
        fold_in, before, packed, image, turned = refs[:2] + refs[2 + skip :]
        fold = fold_in[...]
    fold = jnp.maximum(fold, 1.0)
    left = low_lanes((CXL, 128))
    for a in range(CIL // 4):
        here = slice(a * CXL, (a + 1) * CXL)
        columns = []
        for q in range(4):
            lane = q * (CIL // 4) + a
            columns.append(
                jnp.concatenate(
                    [fold[:, 32 * j + lane : 32 * j + lane + 1] for j in range(3)], axis=0
                )
            )
        for side in range(2):
            lanes = slice(128 * side, 128 * side + 128)
            total = (parts[0][here, lanes] + parts[1][here, lanes]) + (
                parts[2][here, lanes] + parts[3][here, lanes]
            )
            value = total / jnp.where(left, columns[2 * side], columns[2 * side + 1])
            turned[here, lanes] = value
            if half == 0:
                value_out[here, lanes] = value
            else:
                earlier = before[here, lanes]
                even, odd = 2 * side * QUARTER + a * CXL, (2 * side + 1) * QUARTER + a * CXL
                image[even : even + CXL] = jnp.where(left, earlier, swap_lanes(value))
                image[odd : odd + CXL] = jnp.where(left, swap_lanes(earlier), value)
    copy = turned[...].T.astype(jnp.bfloat16)
    for i in range(4):
        packed[256 * i : 256 * i + 256] = copy


def image_call(half, parts, extra, tokens):
    packed = jax.ShapeDtypeStruct((4 * 256, QUARTER), jnp.bfloat16)
    if half == 0:
        out_shape = [
            packed,
            jax.ShapeDtypeStruct((QUARTER, 256), jnp.float32),
            jax.ShapeDtypeStruct((FOLD, 256), jnp.float32),
        ]
    else:
        out_shape = [packed, jax.ShapeDtypeStruct((CELLS, 128), jnp.float32)]
    return pl.pallas_call(
        functools.partial(image_kernel, half, len(tokens)),
        out_shape=out_shape,
        in_specs=[IN_VMEM] * (4 + len(extra)) + [IN_ANY] * len(tokens),
        out_specs=[IN_VMEM] * len(out_shape),
        scratch_shapes=[pltpu.VMEM((QUARTER, 256), jnp.float32)],
        cost_estimate=LIGHT,
        compiler_params=pltpu.CompilerParams(vmem_limit_bytes=VMEM_LIMIT),
        name=f"image_{half}",
    )(*parts, *extra, *tokens)


def read_kernel(spec, order, counts, blocks, cells, own, *refs):
    sizes, first, last, skip, base = spec
    group = 4
    tiles = sum(sizes) // 256
    pieces = refs[: len(sizes)]
    refs = refs[len(sizes) :]
    if last:
        matrices, earlier, refs = refs[0], refs[1], refs[2:]
    if not first:
        before, refs = refs[0], refs[1:]
    refs = refs[skip:]
    out, held, mine, total, live, sems = refs[:6]
    copies = [pltpu.make_async_copy(own, mine, sems.at[0])]
    if not first:
        copies.append(pltpu.make_async_copy(before, total, sems.at[len(sizes) + 1]))
    if last:
        whole_out, earlier_in, band = refs[6:]
        later = [
            pltpu.make_async_copy(earlier, earlier_in, sems.at[len(sizes) + 2]),
            pltpu.make_async_copy(matrices, band, sems.at[len(sizes) + 3]),
        ]
    start = 0
    for i, rows in enumerate(sizes):
        copies.append(
            pltpu.make_async_copy(pieces[i], held.at[pl.ds(start, rows)], sems.at[i + 1])
        )
        start += rows
    for copy in copies:
        copy.start()
    if first:
        total[...] = jnp.zeros_like(total)

    def add_tile(j, n):
        for g in range(8 // group):
            live[n] = order[base + j] * 8 + g * group
            live[n + 128] = j
            n = n + (counts[order[base + j]] > g * group).astype(jnp.int32)
        return n

    if last:
        for copy in later:
            copy.start()
    n = lax.fori_loop(0, tiles, add_tile, 0)
    for copy in copies:
        copy.wait()

    def one_step(step, unused):
        waiting = []
        for k in range(2):
            at = step * 2 + k
            place = jnp.minimum(at, n - 1)
            entry = live[place]
            rows = [
                jnp.where(at < n, cells[pl.ds(entry + i, 1), :], -1) for i in range(group)
            ]
            quarters = [quarter_of(row) for row in rows]
            selector = jnp.concatenate(
                [
                    hot(row - QUARTER * quarter, (QUARTER, 128), 0)
                    for row, quarter in zip(rows, quarters, strict=True)
                ],
                axis=1,
            )
            image = held[pl.ds(pl.multiple_of(live[128 + place] * 256, 256), 256), :]
            got = jnp.dot(image, selector, preferred_element_type=jnp.float32)
            waiting.append((entry, rows, quarters, got))
        for entry, rows, quarters, got in waiting:
            for i in range(group):
                here = pl.ds(pl.multiple_of(blocks[entry + i] * 64, 64), 64)
                part = got[:, 128 * i : 128 * i + 128]
                value = part[:64]
                for q in (1, 2, 3):
                    value = jnp.where(quarters[i] == q, part[64 * q : 64 * q + 64], value)
                sent = jnp.where(rows[i] >= 0, mine[here, :].astype(jnp.float32), 0.0)
                total[here, :] += sent - value
        return 0

    lax.fori_loop(0, (n + 1) // 2, one_step, 0)
    if not last:
        send = pltpu.make_async_copy(total, out, sems.at[len(sizes) + 4])
        send.start()
        send.wait()
        return
    for copy in later:
        copy.wait()
    surveys = matrices.shape[0]
    rows = whole_out.shape[0] // surveys
    sends = []
    for survey in range(surveys):
        for block in range(rows // 128):
            at = survey * (rows // 2) + block * 64
            residual = jnp.concatenate(
                [earlier_in[at : at + 64], total[at : at + 64]], axis=0
            ).T.astype(jnp.bfloat16)
            whole_out[survey * rows + 128 * block : survey * rows + 128 * block + 128] = (
                lax.dot_general(
                    residual,
                    band[survey],
                    (((1,), (1,)), ((), ())),
                    preferred_element_type=jnp.float32,
                )
            )
        sends.append(
            pltpu.make_async_copy(
                whole_out.at[pl.ds(survey * rows, rows)],
                out.at[pl.ds(survey * rows, rows)],
                sems.at[len(sizes) + 4 + survey],
            )
        )
        sends[-1].start()
    for send in sends:
        send.wait()


def read_call(
    order, base, slots, own, pieces, before, matrices=None, earlier=None, tokens=(), cost=None
):
    first, last = before is None, matrices is not None
    sizes = tuple(piece.shape[0] for piece in pieces)
    extra = ([matrices, earlier] if last else []) + ([] if first else [before])
    surveys = matrices.shape[0] if last else 0
    full = (2 * own.shape[0], own.shape[1])
    return pl.pallas_call(
        functools.partial(read_kernel, (sizes, first, last, len(tokens), base)),
        out_shape=jax.ShapeDtypeStruct(full if last else own.shape, jnp.float32),
        in_specs=[IN_SMEM] * 3
        + [IN_VMEM]
        + [IN_HBM] * (1 + len(pieces))
        + [IN_HBM] * len(extra)
        + [IN_ANY] * len(tokens),
        out_specs=IN_HBM,
        scratch_shapes=[
            pltpu.VMEM((sum(sizes), QUARTER), jnp.bfloat16),
            pltpu.VMEM(own.shape, jnp.bfloat16),
            pltpu.VMEM(own.shape, jnp.float32),
            pltpu.SMEM((256,), jnp.int32),
            pltpu.SemaphoreType.DMA((len(sizes) + 5 + surveys,)),
        ]
        + (
            [
                pltpu.VMEM(full, jnp.float32),
                pltpu.VMEM(own.shape, jnp.float32),
                pltpu.VMEM(matrices.shape, jnp.bfloat16),
            ]
            if last
            else []
        ),
        compiler_params=pltpu.CompilerParams(vmem_limit_bytes=VMEM_LIMIT),
        cost_estimate=cost or LIGHT,
        name="read",
    )(order, *slots, own, *pieces, *extra, *tokens)


def with_halo(block, sides, width):
    for axis, count, dim in sides:
        forward = [(i, i + 1) for i in range(count - 1)]
        backward = [(target, source) for source, target in forward]
        low = lax.ppermute(
            lax.slice_in_dim(block, block.shape[dim] - width, None, axis=dim), axis, forward
        )
        high = lax.ppermute(lax.slice_in_dim(block, 0, width, axis=dim), axis, backward)
        block = jnp.concatenate([low, block, high], axis=dim)
    return block


def cycle_box(values, rows_out, cols_out):
    box_total = jnp.zeros((rows_out, cols_out, values.shape[2]), jnp.float32)
    for row_shift in range(3):
        for col_shift in range(3):
            box_total = (
                box_total
                + values[row_shift : row_shift + rows_out, col_shift : col_shift + cols_out]
            )
    return box_total / 9.0


def tensor(padded, il, xl):
    count_il, at_il = il
    count_xl, at_xl = xl
    padded_time = jnp.pad(padded, ((0, 0), (0, 0), (1, 1)))
    grad_il = (padded[2:, 1:-1] - padded[:-2, 1:-1]) * 0.5
    grad_xl = (padded[1:-1, 2:] - padded[1:-1, :-2]) * 0.5
    grad_time = (padded_time[1:-1, 1:-1, 2:] - padded_time[1:-1, 1:-1, :-2]) * 0.5
    rows_il = at_il * CIL + jnp.arange(CIL + 2, dtype=jnp.int32) - 1
    rows_xl = at_xl * CXL + jnp.arange(CXL + 2, dtype=jnp.int32) - 1
    inside_il = ((rows_il >= 0) & (rows_il < CIL * count_il)).astype(jnp.float32)
    inside_xl = ((rows_xl >= 0) & (rows_xl < CXL * count_xl)).astype(jnp.float32)
    cycle_mask = inside_il[:, None, None] * inside_xl[None, :, None]
    factor_pairs = (
        (grad_il, grad_il),
        (grad_xl, grad_xl),
        (grad_time, grad_time),
        (grad_il, grad_xl),
        (grad_il, grad_time),
        (grad_xl, grad_time),
    )
    return jnp.stack(
        [
            cycle_box(left_part * right_part * cycle_mask, CIL, CXL)
            for left_part, right_part in factor_pairs
        ]
    )


def tensor_kernel(place, image, low_il, high_il, low_xl, high_xl, out, padded, boxed):
    padded[:2, 2 : CXL + 2] = low_il[...]
    padded[2 : CIL + 2, 2 : CXL + 2] = image[...]
    padded[CIL + 2 :, 2 : CXL + 2] = high_il[...]
    padded[:, :2] = low_xl[...]
    padded[:, CXL + 2 : CXL + 4] = high_xl[...]
    shape = (CXL + 2, 128)
    col = lax.broadcasted_iota(jnp.int32, shape, 0) + (place[2] * CXL - 1)
    lane = lax.broadcasted_iota(jnp.int32, shape, 1)
    inside = (col >= 0) & (col < CXL * place[3])

    def one_row(r, unused):
        row = place[0] * CIL + r - 1
        here = inside & (row >= 0) & (row < CIL * place[1])
        middle = padded[r + 1, 1 : CXL + 3]
        later = jnp.where(lane < 127, pltpu.roll(middle, 127, 1), 0.0)
        earlier = jnp.where(lane > 0, pltpu.roll(middle, 1, 1), 0.0)
        along = [
            (padded[r + 2, 1 : CXL + 3] - padded[r, 1 : CXL + 3]) * 0.5,
            (padded[r + 1, 2 : CXL + 4] - padded[r + 1, 0 : CXL + 2]) * 0.5,
            (later - earlier) * 0.5,
        ]
        along = [jnp.where(here, part, 0.0) for part in along]
        for k, (i, j) in enumerate(((0, 0), (1, 1), (2, 2), (0, 1), (0, 2), (1, 2))):
            product = along[i] * along[j]
            boxed[k, r] = (product[:CXL] + product[1 : CXL + 1]) + product[2:]
        return 0

    lax.fori_loop(0, CIL + 2, one_row, 0)

    def one_out(r, unused):
        for k in range(6):
            out[k, r] = ((boxed[k, r] + boxed[k, r + 1]) + boxed[k, r + 2]) / 9.0
        return 0

    lax.fori_loop(0, CIL, one_out, 0)


def tensor_call(place, image, halo, tokens=()):
    def kernel(*refs):
        tensor_kernel(*refs[:6], *refs[6 + len(tokens) :])

    return pl.pallas_call(
        kernel,
        out_shape=jax.ShapeDtypeStruct((6, CIL, CXL, 128), jnp.float32),
        in_specs=[IN_SMEM] + [IN_VMEM] * 5 + [IN_ANY] * len(tokens),
        out_specs=IN_VMEM,
        scratch_shapes=[
            pltpu.VMEM((CIL + 4, CXL + 8, 128), jnp.float32),
            pltpu.VMEM((6, CIL + 2, CXL, 128), jnp.float32),
        ],
        compiler_params=pltpu.CompilerParams(vmem_limit_bytes=VMEM_LIMIT),
        cost_estimate=LIGHT,
        name="tensor",
    )(place, image, *halo, *tokens)


def halo_of(image, side_il, side_xl):
    axis_il, count_il = side_il
    axis_xl, count_xl = side_xl
    up_il, up_xl = ([(i, i + 1) for i in range(n - 1)] for n in (count_il, count_xl))
    down_il, down_xl = ([(j, i) for i, j in up] for up in (up_il, up_xl))
    low_il = lax.ppermute(image[-2:], axis_il, up_il)
    high_il = lax.ppermute(image[:2], axis_il, down_il)

    def edge(cols):
        return jnp.concatenate([part[:, cols] for part in (low_il, image, high_il)], axis=0)

    low_xl = lax.ppermute(edge(slice(CXL - 2, CXL)), axis_xl, up_xl)
    high_xl = lax.ppermute(edge(slice(0, 2)), axis_xl, down_xl)
    return low_il, high_il, low_xl, high_xl


SWAP = [(0, 1), (1, 0)]


def along_z(value, step):
    return lax.ppermute(value, "z", [(i, (i + step) % 4) for i in range(4)])


def over(axis, value):
    return lax.ppermute(value, axis, SWAP)


def local_planes(traces, filter_taps, slot_block, slot_cells, pair_count):
    row_block = slot_cells.shape[3]
    capacity = slot_block.shape[2]
    samples = traces.shape[1]
    surveys, tap_count = filter_taps.shape
    x, core, z, y = (lax.axis_index(name) for name in ("x", "c", "z", "y"))
    other = 1 - core

    slot_live = jnp.arange(capacity, dtype=jnp.int32)[None, :] < pair_count[0][:, None]
    out_cells = jnp.where(slot_live[:, :, None], slot_cells[0], -1)
    own_cells = jnp.pad(out_cells, ((0, 0), (0, 1), (0, 0)), constant_values=-1)
    numbers = jnp.concatenate([slot_block[0], pair_count[0][:, None]], axis=1)

    def by_column(value):
        parts = value.reshape((2, 2, 4, 2) + value.shape[1:])
        return jnp.moveaxis(parts, 2, 3).reshape((8, 4) + value.shape[1:])

    arrived = lax.all_to_all(
        jnp.concatenate(
            [
                by_column(own_cells).reshape(8, 32, row_block),
                jnp.pad(by_column(numbers), ((0, 0), (0, 4), (0, row_block - 8))),
            ],
            axis=1,
        ),
        ("x", "c", "y"),
        0,
        0,
        tiled=True,
    )
    own_slots = (pair_count[0], numbers.reshape(256), own_cells.reshape(256, row_block))

    rows_half = traces.shape[0] // 2
    (first_half,) = filter_call(0, traces, filter_taps)
    second_half, matrices = filter_call(1, traces, filter_taps)
    halves = [part.reshape(rows_half, samples) for part in (first_half, second_half)]

    spots = ((x, y), (1 - x, y), (x, 1 - y), (1 - x, 1 - y))
    orders = [lax.rem(z + step, 4) for step in range(4)]
    for at_x, at_y in spots:
        orders += [(at_x * 2 + at_core) * 2 + at_y for at_core in (core, other)]
    wanted = [(spot, core) for spot in spots[:3]] + [(spot, other) for spot in spots[:3]]
    wanted += [(spots[3], core), (spots[3], other)]
    wanted += [(spot, at_core) for spot in spots[:3] for at_core in (core, other)]
    for (at_x, at_y), at_core in wanted:
        orders += [((at_x * 2 + at_core) * 4 + at_z) * 2 + at_y for at_z in range(4)]
    orders = jnp.stack(orders)

    def spread(value, *tokens):
        from_x, from_y, turn_x, turn_y = gate(over("x", value), over("y", value), *tokens)
        return from_x, from_y, (over("y", turn_x), over("x", turn_y))

    def pairs(*pieces):
        return [part for piece in pieces for part in (piece, over("c", piece))]

    def near_stack(half, pieces, tokens=()):
        return stack_call(orders, 4, arrived, pieces, 6, None, 4, half == 0, False, tokens)[0]

    def far_stack(half, parts, before):
        pieces = [*parts, *(over("c", part) for part in parts)]
        return stack_call(orders, 10, arrived, pieces, 2, before, 4, half == 0, True)

    def sum_z(partial):
        return [partial[0]] + [along_z(partial[step], step) for step in (2, 1, 3)]

    def over_z(value):
        return lax.all_to_all(value, "z", 0, 0, tiled=True)

    def read(half, base, pieces, *rest, **named):
        return read_call(orders, base, own_slots, halves[half], pieces, *rest, **named)


    from_x, from_y, parts = spread(halves[0], halves[1], arrived, orders, *own_slots)
    near_0 = near_stack(0, pairs(halves[0], from_x, from_y))
    (own_1,) = tie([halves[1]], near_0)
    halves[1] = own_1
    partial_0 = far_stack(0, tie(parts, near_0), near_0)
    packed_0, stacked, fold = image_call(0, sum_z(partial_0), [], [])
    from_x, from_y, parts = spread(own_1, packed_0)
    columns_0 = over_z(tie([packed_0], from_x)[0])
    near_1 = near_stack(1, pairs(own_1, from_x, from_y))
    partial_1 = far_stack(1, tie(parts, near_1), near_1)
    (columns_0,) = tie([columns_0], partial_1[0])
    from_x, from_y, parts = spread(columns_0)
    own_layers = [columns_0, from_x, from_y]
    residual_0 = read(0, 12, own_layers, None)
    packed_1, image = image_call(1, sum_z(partial_1), [fold, stacked], [residual_0, *parts])
    columns_1 = over_z(packed_1)
    image = image.reshape(CIL, CXL, samples)
    halo = halo_of(image, (("x", "c"), 4), (("z", "y"), 8))
    place = jnp.stack([x * 2 + core, jnp.int32(4), z * 2 + y, jnp.int32(8)])
    own_layers = tie([*own_layers, *parts], packed_1)
    layers = [over("c", layer) for layer in own_layers]
    layers = layers[:3] + list(own_layers[3:]) + layers[3:]
    residual_0 = read(0, 24, layers, residual_0, tokens=[columns_1, *halo])
    structure_tensor = tensor_call(place, image, halo, [residual_0])
    from_x, from_y, parts = spread(columns_1, structure_tensor)
    residual_1 = read(1, 44, pairs(columns_1, from_x, from_y), None)
    parts = tie(parts, residual_1)
    layers = [*parts, *(over("c", part) for part in parts)]
    adjoint_traces = read(1, 36, layers, residual_1, matrices, residual_0)
    return (structure_tensor, adjoint_traces)


def filter_matrices(filter_taps, samples):
    lag_table = (
        jnp.arange(samples, dtype=jnp.int32)[None, :]
        - jnp.arange(samples, dtype=jnp.int32)[:, None]
    )
    tap_count = filter_taps.shape[1]
    inside = (lag_table >= 0) & (lag_table < tap_count)
    picked = filter_taps[:, jnp.clip(lag_table, 0, tap_count - 1)]
    return jnp.where(inside[None], picked, 0.0).astype(jnp.bfloat16)


def local(traces, filter_taps, slot_block, slot_cells, pair_count):
    count_il = lax.axis_size("il")
    count_xl = lax.axis_size("xl")
    devices = count_il * count_xl
    samples = traces.shape[1]
    row_block = slot_cells.shape[3]
    capacity = slot_block.shape[2]
    surveys = filter_taps.shape[0]
    blocks_here = traces.shape[0] // row_block
    cell_count = CIL * CXL
    group_size = 16
    slot_total = devices * capacity
    group_count = slot_total // group_size
    matrices = filter_matrices(filter_taps, samples)
    by_survey = traces.reshape(surveys, blocks_here // surveys * row_block, samples)
    filtered = jnp.einsum("sru,sut->srt", by_survey, matrices, preferred_element_type=jnp.float32)
    filtered = filtered.astype(jnp.bfloat16).reshape(blocks_here, row_block, samples)
    block_ids = slot_block[0].reshape(-1)
    outgoing = jnp.take(filtered, block_ids, axis=0).reshape(devices, capacity, row_block, samples)
    slot_live = jnp.arange(capacity, dtype=jnp.int32)[None, :] < pair_count[0][:, None]
    out_cells = jnp.where(slot_live[:, :, None], slot_cells[0], -1)
    incoming, in_cells = (
        lax.all_to_all(outgoing, ("il", "xl"), split_axis=0, concat_axis=0, tiled=True),
        lax.all_to_all(out_cells, ("il", "xl"), split_axis=0, concat_axis=0, tiled=True),
    )
    incoming = incoming.reshape(slot_total, row_block, samples)
    in_cells = in_cells.reshape(slot_total, row_block)
    cell_line = jnp.arange(cell_count, dtype=jnp.int32)

    def one_hot(group_cells):
        return (cell_line[:, None] == group_cells.reshape(1, -1)).astype(jnp.bfloat16)

    def add_group(running, group_blocks, group_cells):
        stacked, fold_counts = running
        selector = one_hot(group_cells)
        stacked = stacked + jnp.dot(
            selector, group_blocks.reshape(-1, samples), preferred_element_type=jnp.float32
        )
        fold_counts = fold_counts + jnp.sum(selector, axis=1, dtype=jnp.float32)
        return (stacked, fold_counts)

    initial = (jnp.zeros((cell_count, samples), jnp.float32), jnp.zeros((cell_count,), jnp.float32))

    def scan_step(running, scan_item):
        return (add_group(running, scan_item[0], scan_item[1]), None)

    (stacked, fold_counts), unused = lax.scan(
        scan_step,
        initial,
        (
            incoming.reshape(group_count, group_size, row_block, samples),
            in_cells.reshape(group_count, group_size, row_block),
        ),
    )
    stack_image = stacked / jnp.maximum(fold_counts, 1.0)[:, None]
    image_half = stack_image.astype(jnp.bfloat16)

    def read_group(group_cells):
        selector = one_hot(group_cells)
        picked = lax.dot_general(
            selector, image_half, (((0,), (0,)), ((), ())), preferred_element_type=jnp.float32
        )
        return picked.astype(jnp.bfloat16).reshape(group_size, row_block, samples)

    answer = lax.map(read_group, in_cells.reshape(group_count, group_size, row_block)).reshape(
        slot_total, row_block, samples
    )
    returned = lax.all_to_all(
        answer.reshape(devices, capacity, row_block, samples),
        ("il", "xl"),
        split_axis=0,
        concat_axis=0,
        tiled=True,
    )
    returned = returned.reshape(slot_total, row_block, samples)
    out_valid = (out_cells >= 0).reshape(slot_total, row_block, 1)
    zero_half = jnp.zeros((), jnp.bfloat16)
    sent_part = jnp.where(out_valid, outgoing.reshape(slot_total, row_block, samples), zero_half)
    back_part = jnp.where(out_valid, returned, zero_half)
    selector_rows = (
        block_ids[:, None] == jnp.arange(blocks_here, dtype=jnp.int32)[None, :]
    ).astype(jnp.bfloat16)
    residual = jnp.einsum(
        "sb,sit->bit", selector_rows, sent_part, preferred_element_type=jnp.float32
    )
    residual = residual - jnp.einsum(
        "sb,sit->bit", selector_rows, back_part, preferred_element_type=jnp.float32
    )
    residual_half = residual.astype(jnp.bfloat16).reshape(surveys, -1, samples)
    adjoint_traces = jnp.einsum(
        "srt,sut->sru", residual_half, matrices, preferred_element_type=jnp.float32
    ).reshape(traces.shape)
    padded = with_halo(
        stack_image.reshape(CIL, CXL, samples), (("il", count_il, 0), ("xl", count_xl, 1)), 2
    )
    structure_tensor = tensor(
        padded, (count_il, lax.axis_index("il")), (count_xl, lax.axis_index("xl"))
    )
    return (structure_tensor, adjoint_traces)


def solution(mesh):
    inner, names, body = mesh, (("il",), ("xl",)), local
    if mesh.devices.shape == (4, 8):
        inner = Mesh(mesh.devices.reshape(2, 2, 4, 2), ("x", "c", "z", "y"))
        names, body = (("x", "c"), ("z", "y")), local_planes
    il, xl = names
    both = il + xl
    return jax.shard_map(
        body,
        mesh=inner,
        in_specs=(
            P(both, None),
            P(),
            P(both, None, None),
            P(both, None, None, None),
            P(both, None),
        ),
        out_specs=(P(None, il, xl, None), P(both, None)),
        check_vma=False,
    )
```
